512 devices in a mesh: section: 16 (over z, core), tensor: 16 (over y_lo, x), dp: 2 (over y_hi).
Axes of the slice: x: 4, y: 8 (y_hi: 2, y_lo: 4; y = y_hi * 4 + y_lo), z: 8, core: 2. Of those that a mesh axis runs over, the one named last changes fastest.
Arguments:
- enc_hidden: bfloat16 [512, 2048], P(('dp', 'tensor'), 'section'), parts along dimension 0, may hold values from -70 to 70
- mlp_gain: float32 [2048], P('section'), may hold values from 0.25 to 1.75
- final_gain: float32 [2048], P('section'), may hold values from 0.25 to 1.75
- w_gate: bfloat16 [2048, 8192], P('section', 'tensor'), may hold values from -0.125 to 0.125
- w_up: bfloat16 [2048, 8192], P('section', 'tensor'), may hold values from -0.125 to 0.125
- w_down: bfloat16 [8192, 2048], P('tensor', 'section'), may hold values from -0.0625 to 0.0625
- key_weight: bfloat16 [16, 2048, 4096], P('section', None, 'tensor'), may hold values from -0.125 to 0.125
- value_weight: bfloat16 [16, 2048, 4096], P('section', None, 'tensor'), may hold values from -0.125 to 0.125
- queries: bfloat16 [16, 2048, 4096], P('section', 'dp', 'tensor'), parts along dimension 1, may hold values from -340 to 340
- context_grad: bfloat16 [16, 2048, 4096], P('section', 'dp', 'tensor'), parts along dimension 1, may hold values from -6 to 6
Outputs:
- query_grad: bfloat16 [16, 2048, 4096], P('section', 'dp', 'tensor'), parts along dimension 1
- hidden_grad: float32 [512, 2048], P(('dp', 'tensor'), 'section'), parts along dimension 0
- gate_weight_grad: bfloat16 [4096, 8192], P(('dp', 'section'), 'tensor'), parts along dimension 0
- up_weight_grad: bfloat16 [4096, 8192], P(('dp', 'section'), 'tensor'), parts along dimension 0
- down_weight_grad: bfloat16 [16384, 2048], P(('dp', 'tensor'), 'section'), parts along dimension 0
The draws below stay inside these ranges and needn't reach their ends.
There are 2 independent parts, one for each index of `dp`. The reference program is written for one: setup_inputs(seed, part) draws one part's arguments, and reference() takes and returns one part's arrays. A program takes and returns all parts, laid end to end along the dimension named above; an argument that names none is the same for every part. Nothing has to cross between parts.
All inputs are finite; a program needn't handle non-finite values.
Results may differ from the reference program's by a relative error of at most 0.017.
Values may be sent and summed in bfloat16 or wider, within the bound.
No kernel may reach another device: no remote copies, remote signals or barrier semaphores. Data moves between devices by JAX's collectives and lax.ppermute only.
A program may use at most 64 MiB of HBM per device.

```python
import math
import jax
import jax.numpy as jnp
from jax import lax

D = 2048
FF = 8192
HEADS = 16
HEAD = 256
TGT = 1024
SRC = 256
LAYERS = 16
HD = 4096


def draw_enc_hidden(key, part):
    key_base = jax.random.fold_in(key, 11)
    key_rows = jax.random.fold_in(key, 12)
    key_cols = jax.random.fold_in(key, 13)
    col_trend = 1.0 + 2.0 * jnp.arange(D, dtype=jnp.float32)[None, :] / D
    col_scale = col_trend * jnp.exp(jax.random.uniform(key_cols, (1, D), jnp.float32, 0.0, math.log(10.0 / 3.0)))
    row_scale = 0.1 * jnp.exp(jax.random.uniform(key_rows, (SRC, 1), jnp.float32, 0.0, math.log(10.0)))
    base_draw = jnp.clip(jax.random.normal(key_base, (SRC, D), jnp.float32), -6.0, 6.0)
    return (base_draw * row_scale * col_scale).astype(jnp.bfloat16)


def draw_queries(key, part):
    key_base = jax.random.fold_in(key, 21)
    base_draw = jnp.clip(jax.random.normal(key_base, (LAYERS, TGT, HEADS * HEAD), jnp.float32), -6.0, 6.0)
    return base_draw.astype(jnp.bfloat16)


def draw_context_grad(key, part):
    key_base = jax.random.fold_in(key, 31)
    base_draw = jnp.clip(jax.random.normal(key_base, (LAYERS, TGT, HEADS * HEAD), jnp.float32), -6.0, 6.0)
    return base_draw.astype(jnp.bfloat16)


def steps_of(rng, dims, pieces, smallest, largest):
    loudness = 1.0
    for position, parts in pieces:
        steps = jax.random.uniform(jax.random.fold_in(jax.random.fold_in(rng, 6), position), (parts,), jnp.float32, smallest / len(pieces), largest / len(pieces))
        loudness = loudness * jnp.repeat(jnp.exp(steps), dims[position] // parts).reshape((-1,) + (1,) * (len(dims) - 1 - position))
    return loudness


def normal_values(stream_key, shape, deviation, most, pieces=(), kind=jnp.bfloat16):
    loudness = steps_of(stream_key, shape, pieces, -0.22, 0.18) if pieces else 1.0
    result = jax.random.normal(stream_key, shape, jnp.float32) * deviation * loudness
    return jnp.minimum(jnp.maximum(result, -most), most).astype(kind)


def setup_inputs(seed: int = 0, part: int = 0) -> dict:
    splits = jax.random.split(jax.random.key(seed), 11)
    part_keys = jax.random.split(jax.random.fold_in(splits[10], part), 11)
    enc_hidden = draw_enc_hidden(jax.random.fold_in(jax.random.fold_in(splits[10], part), 71), part)
    mlp_gain = jnp.clip(1.0 + 0.15 * jax.random.normal(splits[1], (D,), jnp.float32), 0.25, 1.75)
    final_gain = jnp.clip(1.0 + 0.15 * jax.random.normal(splits[2], (D,), jnp.float32), 0.25, 1.75)
    w_gate = normal_values(splits[3], (D, FF), D ** -0.5, 0.125, ((0, 16), (1, 16)))
    w_up = normal_values(splits[4], (D, FF), D ** -0.5, 0.125, ((0, 16), (1, 16)))
    w_down = normal_values(splits[5], (FF, D), FF ** -0.5, 0.0625, ((0, 16), (1, 16)))
    key_weight = normal_values(splits[6], (LAYERS, D, HD), D ** -0.5, 0.125, ((0, 16), (2, 16)))
    value_weight = normal_values(splits[7], (LAYERS, D, HD), D ** -0.5, 0.125, ((0, 16), (2, 16)))
    queries = draw_queries(jax.random.fold_in(jax.random.fold_in(splits[10], part), 71), part)
    context_grad = draw_context_grad(jax.random.fold_in(jax.random.fold_in(splits[10], part), 71), part)
    return {"enc_hidden": enc_hidden, "mlp_gain": mlp_gain, "final_gain": final_gain, "w_gate": w_gate, "w_up": w_up, "w_down": w_down, "key_weight": key_weight, "value_weight": value_weight, "queries": queries, "context_grad": context_grad}


EPSILON = 1e-06

def layer_pass(encoded, key_matrix, value_matrix, query_block, grad_block):
    scale_factor = HEAD ** (-0.5)
    keys = jnp.dot(encoded, key_matrix, preferred_element_type=jnp.float32).astype(jnp.bfloat16)
    values = jnp.dot(encoded, value_matrix, preferred_element_type=jnp.float32).astype(jnp.bfloat16)
    src_rows = keys.shape[0]
    tgt_rows = query_block.shape[0]
    query_heads = query_block.reshape(tgt_rows, HEADS, HEAD).astype(jnp.float32)
    key_heads = keys.reshape(src_rows, HEADS, HEAD).astype(jnp.float32)
    value_heads = values.reshape(src_rows, HEADS, HEAD).astype(jnp.float32)
    grad_heads = grad_block.reshape(tgt_rows, HEADS, HEAD).astype(jnp.float32)
    scores = jnp.einsum('qhd,khd->hqk', query_heads, key_heads) * scale_factor
    probs = jax.nn.softmax(scores, axis=-1)
    probs_bf = probs.astype(jnp.bfloat16)
    probs_wide = probs_bf.astype(jnp.float32)
    context = jnp.einsum('hqk,khd->qhd', probs_wide, value_heads)
    delta = lax.optimization_barrier(jnp.sum(grad_heads * context, axis=2))
    dprob = jnp.einsum('qhd,khd->hqk', grad_heads, value_heads)
    dscore = (probs * (dprob - jnp.transpose(delta)[:, :, None]) * scale_factor).astype(jnp.bfloat16)
    dscore_wide = dscore.astype(jnp.float32)
    query_grad = jnp.einsum('hqk,khd->qhd', dscore_wide, key_heads).astype(jnp.bfloat16)
    key_grad = jnp.einsum('hqk,qhd->khd', dscore_wide, query_heads).astype(jnp.bfloat16)
    value_grad = jnp.einsum('hqk,qhd->khd', probs_wide, grad_heads).astype(jnp.bfloat16)
    key_grad = key_grad.reshape(src_rows, HEADS * HEAD)
    value_grad = value_grad.reshape(src_rows, HEADS * HEAD)
    contract = (((1,), (1,)), ((), ()))
    encoded_grad = lax.dot_general(key_grad, key_matrix, contract, preferred_element_type=jnp.float32)
    encoded_grad = encoded_grad + lax.dot_general(value_grad, value_matrix, contract, preferred_element_type=jnp.float32)
    return (query_grad.reshape(tgt_rows, HEADS * HEAD), encoded_grad)

def reference(enc_hidden, mlp_gain, final_gain, w_gate, w_up, w_down, key_weight, value_weight, queries, context_grad):
    hidden_wide = enc_hidden.astype(jnp.float32)
    inv_in = lax.rsqrt(lax.optimization_barrier(jnp.mean(hidden_wide * hidden_wide, axis=1, keepdims=True)) + EPSILON)
    normed = (hidden_wide * inv_in * mlp_gain[None, :]).astype(jnp.bfloat16)
    gate_pre = jnp.dot(normed, w_gate, preferred_element_type=jnp.float32)
    up_pre = jnp.dot(normed, w_up, preferred_element_type=jnp.float32)
    sigmoid_gate = jax.nn.sigmoid(gate_pre)
    activated = gate_pre * sigmoid_gate
    hidden_act = (activated * up_pre).astype(jnp.bfloat16)
    outer = hidden_wide + jnp.dot(hidden_act, w_down, preferred_element_type=jnp.float32)
    inv_out = lax.rsqrt(lax.optimization_barrier(jnp.mean(outer * outer, axis=1, keepdims=True)) + EPSILON)
    encoded = (outer * inv_out * final_gain[None, :]).astype(jnp.bfloat16)

    def one_layer(inputs):
        return layer_pass(encoded, inputs[0], inputs[1], inputs[2], inputs[3])
    query_grad, layer_grads = lax.map(one_layer, (key_weight, value_weight, queries, context_grad))
    encoded_grad = lax.optimization_barrier(jnp.sum(layer_grads, axis=0))
    scaled_out = final_gain[None, :] * encoded_grad
    inner_out = lax.optimization_barrier(jnp.mean(scaled_out * outer, axis=1, keepdims=True))
    outer_grad = inv_out * scaled_out - outer * inv_out * inv_out * inv_out * inner_out
    outer_grad_bf = outer_grad.astype(jnp.bfloat16)
    rows_contract = (((0,), (0,)), ((), ()))
    down_weight_grad = lax.dot_general(hidden_act, outer_grad_bf, rows_contract, preferred_element_type=jnp.float32).astype(jnp.bfloat16)
    cols_contract = (((1,), (1,)), ((), ()))
    act_grad = lax.dot_general(outer_grad_bf, w_down, cols_contract, preferred_element_type=jnp.float32)
    up_grad = (act_grad * activated).astype(jnp.bfloat16)
    gate_grad = (act_grad * up_pre * sigmoid_gate * (1.0 + gate_pre * (1.0 - sigmoid_gate))).astype(jnp.bfloat16)
    gate_weight_grad = lax.dot_general(normed, gate_grad, rows_contract, preferred_element_type=jnp.float32).astype(jnp.bfloat16)
    up_weight_grad = lax.dot_general(normed, up_grad, rows_contract, preferred_element_type=jnp.float32).astype(jnp.bfloat16)
    normed_grad = lax.dot_general(gate_grad, w_gate, cols_contract, preferred_element_type=jnp.float32)
    normed_grad = normed_grad + lax.dot_general(up_grad, w_up, cols_contract, preferred_element_type=jnp.float32)
    scaled_in = mlp_gain[None, :] * normed_grad
    inner_in = lax.optimization_barrier(jnp.mean(scaled_in * hidden_wide, axis=1, keepdims=True))
    hidden_grad = outer_grad + inv_in * scaled_in - hidden_wide * inv_in * inv_in * inv_in * inner_in
    return (query_grad, hidden_grad, gate_weight_grad, up_weight_grad, down_weight_grad)
```

```python
import jax
import jax.numpy as jnp
from jax import lax
from jax.experimental import pallas as pl
from jax.experimental.pallas import tpu as pltpu
from jax.sharding import Mesh
from jax.sharding import PartitionSpec as P

D = 2048
HEAD = 256
LANES = 128
EPSILON = 1e-06
BF = jnp.bfloat16
F32 = jnp.float32

ROWS = (((0,), (0,)), ((), ()))
COLS = (((1,), (1,)), ((), ()))
SECTION = ("z", "core")


def exchange(pieces, axis):
    return lax.all_to_all(pieces, axis, split_axis=0, concat_axis=0, tiled=True)


def sent_to_all(value, axis):
    return exchange(jnp.broadcast_to(value, (lax.axis_size(axis), *value.shape)), axis)


def other_core(value):
    return lax.ppermute(value, "core", [(0, 1), (1, 0)])


def high_low(value):
    high = lax.reduce_precision(value, 8, 7)
    return high.astype(BF), (value - high).astype(BF)


def attend(core_ref, mine_ref, other_ref, wk_ref, wv_ref, recip_ref, q_ref, g_ref, qg_ref, keep_ref, send_ref):
    core = core_ref[0]
    pairs = mine_ref.shape[0]
    rows = mine_ref.shape[1]
    scale = HEAD ** (-0.5)
    keys_raw = jnp.zeros((rows, HEAD), F32)
    values_raw = jnp.zeros((rows, HEAD), F32)
    square = jnp.zeros((rows, 1), F32)
    for z in range(pairs):
        for block_ref, side in ((mine_ref, core), (other_ref, 1 - core)):
            block = block_ref[z]
            keys_raw += jnp.dot(block, wk_ref[z, side], preferred_element_type=F32)
            values_raw += jnp.dot(block, wv_ref[z, side], preferred_element_type=F32)
            wide = block.astype(F32) * recip_ref[z, side]
            square += jnp.sum(wide * wide, axis=1, keepdims=True)
    inv_out = lax.rsqrt(square / D + EPSILON)
    keys = (keys_raw * inv_out).astype(BF)
    values = (values_raw * inv_out).astype(BF)
    key_grad = jnp.zeros((rows, HEAD), F32)
    value_grad = jnp.zeros((rows, HEAD), F32)
    step = 256
    for at in range(0, q_ref.shape[0], step):
        query = q_ref[at : at + step, :]
        grad = g_ref[at : at + step, :]
        scores = lax.dot_general(keys, query, COLS, preferred_element_type=F32) * scale
        raised = jnp.exp(scores - jnp.max(scores, axis=0, keepdims=True))
        probs = raised / jnp.sum(raised, axis=0, keepdims=True)
        probs_bf = probs.astype(BF)
        dprob = lax.dot_general(values, grad, COLS, preferred_element_type=F32)
        delta = jnp.sum(probs_bf.astype(F32) * dprob, axis=0, keepdims=True)
        dscore = (probs * (dprob - delta) * scale).astype(BF)
        qg_ref[at : at + step, :] = lax.dot_general(
            dscore, keys, ROWS, preferred_element_type=F32
        ).astype(BF)
        key_grad += jnp.dot(dscore, query, preferred_element_type=F32)
        value_grad += jnp.dot(probs_bf, grad, preferred_element_type=F32)
    key_grad = key_grad.astype(BF)
    value_grad = value_grad.astype(BF)
    inner = jnp.sum(
        key_grad.astype(F32) * keys_raw + value_grad.astype(F32) * values_raw, axis=1, keepdims=True
    )
    along = inv_out * inv_out * inv_out * inner * (1.0 / D)
    for z in range(pairs):
        for block_ref, out_ref, side in ((mine_ref, keep_ref, core), (other_ref, send_ref, 1 - core)):
            total = lax.dot_general(key_grad, wk_ref[z, side], COLS, preferred_element_type=F32)
            total += lax.dot_general(value_grad, wv_ref[z, side], COLS, preferred_element_type=F32)
            recip = recip_ref[z, side]
            term = inv_out * total - block_ref[z].astype(F32) * (recip * recip) * along
            out_ref[z] = term.astype(out_ref.dtype)


def cross_attention(mine, other, key_matrix, value_matrix, gain_all, query, grad):
    pairs = mine.shape[0]
    blocks = (pairs, 2, LANES, HEAD)
    recip = (1.0 / gain_all).reshape(pairs, 2, 1, LANES)
    core = lax.axis_index("core").astype(jnp.int32).reshape(1)
    vmem = pl.BlockSpec(memory_space=pltpu.VMEM)
    return pl.pallas_call(
        attend,
        out_shape=(
            jax.ShapeDtypeStruct(query.shape, BF),
            jax.ShapeDtypeStruct(mine.shape, F32),
            jax.ShapeDtypeStruct(mine.shape, BF),
        ),
        in_specs=[pl.BlockSpec(memory_space=pltpu.SMEM)] + [vmem] * 7,
        out_specs=(vmem, vmem, vmem),
        compiler_params=pltpu.CompilerParams(vmem_limit_bytes=40 * 1024 * 1024),
        cost_estimate=pl.CostEstimate(
            flops=3_500_000_000, bytes_accessed=8_000_000, transcendentals=262144
        ),
    )(core, mine, other, key_matrix.reshape(blocks), value_matrix.reshape(blocks), recip, query, grad)


def on_device(
    enc_hidden,
    mlp_gain,
    final_gain,
    w_gate,
    w_up,
    w_down,
    key_weight,
    value_weight,
    queries,
    context_grad,
):
    block, feats = enc_hidden.shape
    width = w_gate.shape[1]
    hidden_all = sent_to_all(enc_hidden, "tensor").reshape(-1, feats)
    tokens = hidden_all.shape[0]
    hidden_all_wide = hidden_all.astype(F32)
    scaled_all = (hidden_all_wide * mlp_gain[None, :]).astype(BF)
    gate_part = jnp.dot(scaled_all, w_gate, preferred_element_type=F32).astype(BF)
    up_part = jnp.dot(scaled_all, w_up, preferred_element_type=F32).astype(BF)
    square = jnp.sum(hidden_all_wide * hidden_all_wide, axis=1).reshape(-1, 1, block)
    groups = square.shape[0]
    gain_1 = lax.reduce_precision(final_gain, 8, 7)
    gain_2 = lax.reduce_precision(final_gain - gain_1, 8, 7)
    gain_3 = final_gain - gain_1 - gain_2
    gains = jnp.stack([gain_1, gain_2, gain_3]).astype(BF)
    gains = jnp.broadcast_to(gains, (groups, 3, LANES))
    squares = jnp.concatenate(high_low(square), axis=1)
    squares = jnp.pad(squares, ((0, 0), (0, 0), (0, LANES - block)))
    extra = jnp.pad(jnp.concatenate([gains, squares], axis=1), ((0, 0), (0, block - 5), (0, 0)))
    pieces = jnp.concatenate(
        [gate_part.reshape(groups, block, width), up_part.reshape(groups, block, width), extra], axis=2
    )
    arrived = exchange(pieces, SECTION).astype(F32)
    gain_all = jnp.sum(arrived[:, :3, 2 * width :], axis=1).reshape(-1)
    square_in = jnp.sum(arrived[:, 3:5, 2 * width : 2 * width + block], axis=(0, 1))
    gate_up = jnp.sum(arrived[:, :, : 2 * width], axis=0)
    inv_in = lax.rsqrt(square_in / D + EPSILON)[:, None]
    gate_pre = gate_up[:, :width] * inv_in
    up_pre = gate_up[:, width:] * inv_in
    sigmoid_gate = jax.nn.sigmoid(gate_pre)
    activated = gate_pre * sigmoid_gate
    hidden_act = (activated * up_pre).astype(BF)
    act_all = sent_to_all(hidden_act, SECTION).reshape(tokens, width)
    mixed_part = jnp.dot(act_all, w_down, preferred_element_type=F32).astype(BF)
    mixed = exchange(mixed_part.reshape(groups, block, feats), "tensor").astype(F32).sum(axis=0)
    outer = enc_hidden.astype(F32) + mixed
    scaled_outer = (outer * final_gain[None, :]).astype(BF)
    mine = sent_to_all(scaled_outer, ("z", "tensor")).reshape(-1, tokens, feats)
    other = other_core(mine)
    query_grad, keep, send = cross_attention(
        mine, other, key_weight[0], value_weight[0], gain_all, queries[0], context_grad[0]
    )
    both = (keep + other_core(send).astype(F32)).astype(BF)
    both = exchange(both.reshape(-1, block, feats), ("z", "tensor")).astype(F32).sum(axis=0)
    outer_grad = both * final_gain[None, :]
    outer_all = sent_to_all(outer_grad.astype(BF), "tensor").reshape(tokens, feats)
    act_part = lax.dot_general(outer_all, w_down, COLS, preferred_element_type=F32).astype(BF)
    act_grad = exchange(act_part.reshape(groups, block, width), SECTION).astype(F32).sum(axis=0)
    down_weight_grad = lax.dot_general(
        act_all, outer_all, ROWS, preferred_element_type=F32
    ).astype(BF)
    up_grad = act_grad * activated
    gate_grad = act_grad * up_pre * sigmoid_gate * (1.0 + gate_pre * (1.0 - sigmoid_gate))
    inner = jnp.sum(gate_grad * gate_pre + up_grad * up_pre, axis=1, keepdims=True)
    inner = inner * inv_in * inv_in / D
    inner = jnp.pad(jnp.concatenate(high_low(inner), axis=1), ((0, 0), (0, LANES - 2)))
    grads = jnp.concatenate(
        [(gate_grad * inv_in).astype(BF), (up_grad * inv_in).astype(BF), inner], axis=1
    )
    grads = sent_to_all(grads, SECTION).reshape(tokens, 2 * width + LANES)
    gate_all = grads[:, :width]
    up_all = grads[:, width : 2 * width]
    inner_all = jnp.sum(grads[:, 2 * width : 2 * width + 2].astype(F32), axis=1, keepdims=True)
    normed_grad = lax.dot_general(gate_all, w_gate, COLS, preferred_element_type=F32)
    normed_grad += lax.dot_general(up_all, w_up, COLS, preferred_element_type=F32)
    part = (normed_grad * mlp_gain[None, :] - hidden_all_wide * inner_all).astype(BF)
    part = exchange(part.reshape(groups, block, feats), "tensor").astype(F32).sum(axis=0)
    gate_weight_grad = lax.dot_general(
        scaled_all, gate_all, ROWS, preferred_element_type=F32
    ).astype(BF)
    up_weight_grad = lax.dot_general(
        scaled_all, up_all, ROWS, preferred_element_type=F32
    ).astype(BF)
    hidden_grad = outer_grad + part
    return (query_grad[None], hidden_grad, gate_weight_grad, up_weight_grad, down_weight_grad)


def solution(mesh):
    names = list(mesh.axis_names)
    at = names.index("section")
    shape = list(mesh.devices.shape)
    names[at : at + 1] = SECTION
    shape[at : at + 1] = [shape[at] // 2, 2]
    fine = Mesh(mesh.devices.reshape(shape), tuple(names))
    in_specs = (
        P(("dp", "tensor"), SECTION),
        P(SECTION),
        P(SECTION),
        P(SECTION, "tensor"),
        P(SECTION, "tensor"),
        P("tensor", SECTION),
        P(SECTION, None, "tensor"),
        P(SECTION, None, "tensor"),
        P(SECTION, "dp", "tensor"),
        P(SECTION, "dp", "tensor"),
    )
    out_specs = (
        P(SECTION, "dp", "tensor"),
        P(("dp", "tensor"), SECTION),
        P(("dp", *SECTION), "tensor"),
        P(("dp", *SECTION), "tensor"),
        P(("dp", "tensor"), SECTION),
    )
    return jax.shard_map(
        on_device, mesh=fine, in_specs=in_specs, out_specs=out_specs, check_vma=False
    )
```

```python
import jax
import jax.numpy as jnp
from jax import lax
from jax.experimental import pallas as pl
from jax.experimental.pallas import tpu as pltpu
from jax.sharding import Mesh
from jax.sharding import PartitionSpec as P

D = 2048
HEAD = 256
LANES = 128
EPSILON = 1e-06
BF = jnp.bfloat16
F32 = jnp.float32

ROWS = (((0,), (0,)), ((), ()))
COLS = (((1,), (1,)), ((), ()))
SECTION = ("z", "core")


def exchange(pieces, axis):
    return lax.all_to_all(pieces, axis, split_axis=0, concat_axis=0, tiled=True)


def sent_to_all(value, axis):
    return exchange(jnp.broadcast_to(value, (lax.axis_size(axis), *value.shape)), axis)


def other_core(value):
    return lax.ppermute(value, "core", [(0, 1), (1, 0)])


def high_low(value):
    high = lax.reduce_precision(value, 8, 7)
    return high.astype(BF), (value - high).astype(BF)


def attend(core_ref, mine_ref, other_ref, wk_ref, wv_ref, recip_ref, q_ref, g_ref, qg_ref, keep_ref, send_ref):
    core = core_ref[0]
    pairs = mine_ref.shape[0]
    rows = mine_ref.shape[1]
    scale = HEAD ** (-0.5)
    keys_raw = jnp.zeros((rows, HEAD), F32)
    values_raw = jnp.zeros((rows, HEAD), F32)
    square = jnp.zeros((rows, 1), F32)
    for z in range(pairs):
        for block_ref, side in ((mine_ref, core), (other_ref, 1 - core)):
            block = block_ref[z]
            keys_raw += jnp.dot(block, wk_ref[z, side], preferred_element_type=F32)
            values_raw += jnp.dot(block, wv_ref[z, side], preferred_element_type=F32)
            wide = block.astype(F32) * recip_ref[z, side]
            square += jnp.sum(wide * wide, axis=1, keepdims=True)
    inv_out = lax.rsqrt(square / D + EPSILON)
    keys = (keys_raw * inv_out).astype(BF)
    values = (values_raw * inv_out).astype(BF)
    key_grad = jnp.zeros((rows, HEAD), F32)
    value_grad = jnp.zeros((rows, HEAD), F32)
    step = 256
    for at in range(0, q_ref.shape[0], step):
        query = q_ref[at : at + step, :]
        grad = g_ref[at : at + step, :]
        scores = lax.dot_general(keys, query, COLS, preferred_element_type=F32) * scale
        raised = jnp.exp(scores - jnp.max(scores, axis=0, keepdims=True))
        probs = raised / jnp.sum(raised, axis=0, keepdims=True)
        probs_bf = probs.astype(BF)
        dprob = lax.dot_general(values, grad, COLS, preferred_element_type=F32)
        delta = jnp.sum(probs_bf.astype(F32) * dprob, axis=0, keepdims=True)
        dscore = (probs * (dprob - delta) * scale).astype(BF)
        qg_ref[at : at + step, :] = lax.dot_general(
            dscore, keys, ROWS, preferred_element_type=F32
        ).astype(BF)
        key_grad += jnp.dot(dscore, query, preferred_element_type=F32)
        value_grad += jnp.dot(probs_bf, grad, preferred_element_type=F32)
    key_grad = key_grad.astype(BF)
    value_grad = value_grad.astype(BF)
    inner = jnp.sum(
        key_grad.astype(F32) * keys_raw + value_grad.astype(F32) * values_raw, axis=1, keepdims=True
    )
    along = inv_out * inv_out * inv_out * inner * (1.0 / D)
    first = core == 0
    for z in range(pairs):
        for side in range(2):
            block = jnp.where(core == side, mine_ref[z], other_ref[z]).astype(F32)
            total = lax.dot_general(key_grad, wk_ref[z, side], COLS, preferred_element_type=F32)
            total += lax.dot_general(value_grad, wv_ref[z, side], COLS, preferred_element_type=F32)
            recip = recip_ref[z, side]
            term = inv_out * total - block * (recip * recip) * along
            term = term.reshape(pairs, 2, -1, LANES)
            keep_ref[:, 2 * z + side] = jnp.where(first, term[:, 0], term[:, 1])
            send_ref[:, 2 * z + side] = jnp.where(first, term[:, 1], term[:, 0]).astype(BF)


def cross_attention(mine, other, key_matrix, value_matrix, gain_all, query, grad):
    pairs = mine.shape[0]
    blocks = (pairs, 2, LANES, HEAD)
    split = (pairs, 2 * pairs, mine.shape[1] // (2 * pairs), LANES)
    recip = (1.0 / gain_all).reshape(pairs, 2, 1, LANES)
    core = lax.axis_index("core").astype(jnp.int32).reshape(1)
    vmem = pl.BlockSpec(memory_space=pltpu.VMEM)
    return pl.pallas_call(
        attend,
        out_shape=(
            jax.ShapeDtypeStruct(query.shape, BF),
            jax.ShapeDtypeStruct(split, F32),
            jax.ShapeDtypeStruct(split, BF),
        ),
        in_specs=[pl.BlockSpec(memory_space=pltpu.SMEM)] + [vmem] * 7,
        out_specs=(vmem, vmem, vmem),
        compiler_params=pltpu.CompilerParams(vmem_limit_bytes=40 * 1024 * 1024),
        cost_estimate=pl.CostEstimate(
            flops=3_500_000_000, bytes_accessed=8_000_000, transcendentals=262144
        ),
    )(core, mine, other, key_matrix.reshape(blocks), value_matrix.reshape(blocks), recip, query, grad)


def on_device(
    enc_hidden,
    mlp_gain,
    final_gain,
    w_gate,
    w_up,
    w_down,
    key_weight,
    value_weight,
    queries,
    context_grad,
):
    block, feats = enc_hidden.shape
    width = w_gate.shape[1]
    gate_full = lax.all_gather(w_gate, SECTION, axis=0, tiled=True)
    up_full = lax.all_gather(w_up, SECTION, axis=0, tiled=True)
    down_full = lax.all_gather(w_down, SECTION, axis=0)
    hidden_all = sent_to_all(enc_hidden, "tensor").reshape(-1, feats)
    tokens = hidden_all.shape[0]
    hidden_all_wide = hidden_all.astype(F32)
    scaled_all = (hidden_all_wide * mlp_gain[None, :]).astype(BF)
    gate_part = jnp.dot(scaled_all, w_gate, preferred_element_type=F32).astype(BF)
    up_part = jnp.dot(scaled_all, w_up, preferred_element_type=F32).astype(BF)
    square = jnp.sum(hidden_all_wide * hidden_all_wide, axis=1).reshape(-1, 1, block)
    groups = square.shape[0]
    gains = jnp.stack([final_gain, mlp_gain])
    gain_1 = lax.reduce_precision(gains, 8, 7)
    gain_2 = lax.reduce_precision(gains - gain_1, 8, 7)
    gain_3 = gains - gain_1 - gain_2
    gains = jnp.concatenate([gain_1, gain_2, gain_3]).astype(BF)
    gains = jnp.broadcast_to(gains, (groups, 6, LANES))
    squares = jnp.concatenate(high_low(square), axis=1)
    squares = jnp.pad(squares, ((0, 0), (0, 0), (0, LANES - block)))
    extra = jnp.pad(jnp.concatenate([gains, squares], axis=1), ((0, 0), (0, block - 8), (0, 0)))
    pieces = jnp.concatenate(
        [gate_part.reshape(groups, block, width), up_part.reshape(groups, block, width), extra], axis=2
    )
    arrived = exchange(pieces, SECTION).astype(F32)
    gain_all = arrived[:, 0:2, 2 * width :] + arrived[:, 2:4, 2 * width :]
    gain_all = gain_all + arrived[:, 4:6, 2 * width :]
    square_in = jnp.sum(arrived[:, 6:8, 2 * width : 2 * width + block], axis=(0, 1))
    gate_up = jnp.sum(arrived[:, :, : 2 * width], axis=0)
    inv_in = lax.rsqrt(square_in / D + EPSILON)[:, None]
    gate_pre = gate_up[:, :width] * inv_in
    up_pre = gate_up[:, width:] * inv_in
    sigmoid_gate = jax.nn.sigmoid(gate_pre)
    activated = gate_pre * sigmoid_gate
    hidden_act = (activated * up_pre).astype(BF)
    act_all = sent_to_all(hidden_act, SECTION).reshape(tokens, width)
    mixed_part = jnp.dot(act_all, w_down, preferred_element_type=F32).astype(BF)
    mixed = exchange(mixed_part.reshape(groups, block, feats), "tensor").astype(F32).sum(axis=0)
    outer = enc_hidden.astype(F32) + mixed
    scaled_outer = (outer * final_gain[None, :]).astype(BF)
    mine = sent_to_all(scaled_outer, ("z", "tensor")).reshape(-1, tokens, feats)
    other = other_core(mine)
    query_grad, keep, send = cross_attention(
        mine, other, key_weight[0], value_weight[0], gain_all[:, 0], queries[0], context_grad[0]
    )
    both = (keep + other_core(send).astype(F32)).astype(BF)
    both = exchange(both.reshape(-1, block, feats), ("z", "tensor")).astype(F32).sum(axis=0)
    gains_here = lax.dynamic_index_in_dim(gain_all, lax.axis_index("tensor"), 0, keepdims=False)
    outer_grad = both * gains_here[:1]
    outer_row = sent_to_all(outer_grad.astype(BF), "tensor")
    act_grad = jnp.einsum("btf,bhf->th", outer_row, down_full, preferred_element_type=F32)
    outer_all = exchange(outer_row, SECTION).reshape(tokens, feats)
    down_weight_grad = lax.dot_general(
        act_all, outer_all, ROWS, preferred_element_type=F32
    ).astype(BF)
    up_grad = act_grad * activated
    gate_grad = act_grad * up_pre * sigmoid_gate * (1.0 + gate_pre * (1.0 - sigmoid_gate))
    inner = jnp.sum(gate_grad * gate_pre + up_grad * up_pre, axis=1)[None, :]
    inner = inner * (inv_in * inv_in / D).reshape(1, -1)
    inner = jnp.concatenate(high_low(inner), axis=0)
    inner = jnp.pad(inner, ((0, 6), (0, LANES - block)))
    gate_grad = (gate_grad * inv_in).astype(BF)
    up_grad = (up_grad * inv_in).astype(BF)
    normed_grad = lax.dot_general(gate_grad, gate_full, COLS, preferred_element_type=F32)
    normed_grad += lax.dot_general(up_grad, up_full, COLS, preferred_element_type=F32)
    part = jnp.swapaxes(normed_grad.astype(BF).reshape(block, groups, feats), 0, 1)
    part = jnp.concatenate([part, jnp.broadcast_to(inner, (groups, *inner.shape))], axis=1)
    part = exchange(part, "tensor").astype(F32).sum(axis=0)
    along = part[block : block + 1] + part[block + 1 : block + 2]
    final = jnp.concatenate(
        [outer_grad + gains_here[1:] * part[:block], jnp.pad(along, ((0, 7), (0, 0)))], axis=0
    )
    swap = [(a * groups + b, b * groups + a) for a in range(groups) for b in range(groups)]
    final = lax.ppermute(final, (*SECTION, "tensor"), swap)
    hidden_grad = final[:block] - enc_hidden.astype(F32) * final[block, :block][:, None]
    grads = sent_to_all(jnp.concatenate([gate_grad, up_grad], axis=1), SECTION)
    grads = grads.reshape(tokens, 2 * width)
    gate_weight_grad = lax.dot_general(
        scaled_all, grads[:, :width], ROWS, preferred_element_type=F32
    ).astype(BF)
    up_weight_grad = lax.dot_general(
        scaled_all, grads[:, width:], ROWS, preferred_element_type=F32
    ).astype(BF)
    return (query_grad[None], hidden_grad, gate_weight_grad, up_weight_grad, down_weight_grad)


def solution(mesh):
    names = list(mesh.axis_names)
    at = names.index("section")
    shape = list(mesh.devices.shape)
    names[at : at + 1] = SECTION
    shape[at : at + 1] = [shape[at] // 2, 2]
    fine = Mesh(mesh.devices.reshape(shape), tuple(names))
    in_specs = (
        P(("dp", "tensor"), SECTION),
        P(SECTION),
        P(SECTION),
        P(SECTION, "tensor"),
        P(SECTION, "tensor"),
        P("tensor", SECTION),
        P(SECTION, None, "tensor"),
        P(SECTION, None, "tensor"),
        P(SECTION, "dp", "tensor"),
        P(SECTION, "dp", "tensor"),
    )
    out_specs = (
        P(SECTION, "dp", "tensor"),
        P(("dp", "tensor"), SECTION),
        P(("dp", *SECTION), "tensor"),
        P(("dp", *SECTION), "tensor"),
        P(("dp", "tensor"), SECTION),
    )
    return jax.shard_map(
        on_device, mesh=fine, in_specs=in_specs, out_specs=out_specs, check_vma=False
    )
```

```python
import jax
import jax.numpy as jnp
from jax import lax
from jax.experimental import pallas as pl
from jax.experimental.pallas import tpu as pltpu
from jax.sharding import Mesh
from jax.sharding import PartitionSpec as P

D = 2048
HEAD = 256
LANES = 128
EPSILON = 1e-06
BF = jnp.bfloat16
F32 = jnp.float32

ROWS = (((0,), (0,)), ((), ()))
COLS = (((1,), (1,)), ((), ()))
SECTION = ("z", "core")
WIDE = ("core", "tensor")


def exchange(pieces, axis):
    return lax.all_to_all(pieces, axis, split_axis=0, concat_axis=0, tiled=True)


def other_core(value):
    return lax.ppermute(value, "core", [(0, 1), (1, 0)])


def dot(left, right, dims=(((1,), (0,)), ((), ()))):
    return lax.dot_general(left, right, dims, preferred_element_type=F32)


def in_thirds(value):
    high = value.astype(BF).astype(F32)
    middle = (value - high).astype(BF).astype(F32)
    return high, middle, value - high - middle


def in_two_lanes(column):
    lane = lax.broadcasted_iota(jnp.int32, (column.shape[0], LANES), 1)
    high = column.astype(BF).astype(F32)
    return jnp.where(lane == 0, high, jnp.where(lane == 1, column - high, 0.0)).astype(BF)


def from_two_lanes(tile):
    lane = lax.broadcasted_iota(jnp.int32, tile.shape, 1)
    return jnp.sum(jnp.where(lane < 2, tile, 0.0), axis=1, keepdims=True)


def half_of(core, half):
    return pl.ds(pl.multiple_of(core * half, half), half)


def start(core_ref, x_ref, mlp_ref, final_ref, gate_ref, up_ref, down_ref, copies_ref, sent_ref):
    half = gate_ref.shape[1] // 2
    feats = gate_ref.shape[0]
    quarter = half // 4
    there = half_of(1 - core_ref[0], half)
    for i in range(copies_ref.shape[0]):
        copies_ref[i] = x_ref[...]
    sent_ref[:feats, :half] = gate_ref[:, there]
    sent_ref[:feats, half:] = up_ref[:, there]
    for i in range(4):
        at = pl.ds(pl.multiple_of((1 - core_ref[0]) * half + i * quarter, quarter), quarter)
        sent_ref[feats : feats + quarter, i * LANES : (i + 1) * LANES] = down_ref[at, :]
    row = lax.broadcasted_iota(jnp.int32, (16, LANES), 0)
    thirds = zip(in_thirds(mlp_ref[...]), in_thirds(final_ref[...]))
    for i, (mlp, final) in enumerate(thirds):
        tile = jnp.where(row == 0, mlp, jnp.where(row == 1, final, 0.0))
        sent_ref[feats + quarter :, i * LANES : (i + 1) * LANES] = tile.astype(BF)
    sent_ref[feats + quarter :, 3 * LANES :] = jnp.zeros((16, LANES), BF)


def got_gains(got_ref, rows):
    tile = got_ref[rows : rows + 16, :].astype(F32)
    tile = tile[:, :LANES] + tile[:, LANES : 2 * LANES] + tile[:, 2 * LANES : 3 * LANES]
    return tile[0:1], tile[1:2]


def gate_up(core_ref, x_ref, mlp_ref, gate_ref, up_ref, got_ref, pieces_ref, scaled_ref):
    core = core_ref[0]
    half = gate_ref.shape[1] // 2
    feats = gate_ref.shape[0]
    here = half_of(core, half)
    x_here = x_ref[core].astype(F32)
    x_there = x_ref[1 - core].astype(F32)
    scaled = (x_here * mlp_ref[...]).astype(BF)
    scaled_ref[...] = scaled
    mlp_there, _ = got_gains(got_ref, feats + half // 4)
    scaled_there = (x_there * mlp_there).astype(BF)
    gate = dot(scaled, gate_ref[:, here]) + dot(scaled_there, got_ref[:feats, :half])
    up = dot(scaled, up_ref[:, here]) + dot(scaled_there, got_ref[:feats, half:])
    square = jnp.sum(x_here * x_here + x_there * x_there, axis=1, keepdims=True)
    shape = pieces_ref.shape[:2]
    pieces_ref[:, :, :half] = gate.astype(BF).reshape(*shape, half)
    pieces_ref[:, :, half : 2 * half] = up.astype(BF).reshape(*shape, half)
    pieces_ref[:, :, 2 * half :] = in_two_lanes(square).reshape(*shape, LANES)


def activate(core_ref, arrived_ref, final_ref, got_ref, copies_ref, gate_f_ref, up_f_ref, inner_f_ref):
    core = core_ref[0]
    pieces, share, half = copies_ref.shape
    share = share - 16
    total = arrived_ref[0].astype(F32)
    for i in range(1, pieces):
        total += arrived_ref[i].astype(F32)
    inv = lax.rsqrt(from_two_lanes(total[:, 2 * half :]) * (1.0 / D) + EPSILON)
    gate_pre = total[:, :half] * inv
    up_pre = total[:, half : 2 * half] * inv
    sigmoid_gate = jax.nn.sigmoid(gate_pre)
    activated = gate_pre * sigmoid_gate
    hidden_act = (activated * up_pre).astype(BF)
    gate_factor = up_pre * sigmoid_gate * (1.0 + gate_pre * (1.0 - sigmoid_gate))
    gate_f_ref[...] = gate_factor * inv
    up_f_ref[...] = activated * inv
    inner_f_ref[...] = (gate_factor * gate_pre + activated * up_pre) * (inv * inv * (1.0 / D))
    _, final_there = got_gains(got_ref, got_ref.shape[0] - 16)
    final_here = final_ref[...]
    first = core == 0
    low = in_thirds(jnp.where(first, final_here, final_there))
    high = in_thirds(jnp.where(first, final_there, final_here))
    row = lax.broadcasted_iota(jnp.int32, (16, LANES), 0)
    tiles = []
    for parts in (low, high):
        tile = jnp.where(row == 0, parts[0], jnp.where(row == 1, parts[1], 0.0))
        tiles.append(jnp.where(row == 2, parts[2], tile).astype(BF))
    gains = jnp.concatenate(tiles, axis=1)
    for i in range(pieces):
        copies_ref[i, :share] = hidden_act
        copies_ref[i, share:] = gains


def down_half(got_ref, feats, half):
    quarter = half // 4
    rows = got_ref[feats : feats + quarter, :]
    return jnp.concatenate([rows[:, i * LANES : (i + 1) * LANES] for i in range(4)], axis=0)


def mix(core_ref, act_ref, down_ref, got_ref, pieces_ref, recip_ref):
    core = core_ref[0]
    pieces, share, half = act_ref.shape
    share = share - 16
    feats = down_ref.shape[1]
    act = act_ref[:, :share].reshape(pieces * share, half)
    shape = pieces_ref.shape[1:]
    here = dot(act, down_ref[half_of(core, half), :])
    pieces_ref[core] = here.astype(BF).reshape(shape)
    there = dot(act, down_half(got_ref, feats, half))
    pieces_ref[1 - core] = there.astype(BF).reshape(shape)
    for z in range(pieces):
        tile = act_ref[z, share:].astype(F32)
        recip = 1.0 / (tile[0:1] + tile[1:2] + tile[2:3])
        recip_ref[z, 0] = recip[:, :LANES]
        recip_ref[z, 1] = recip[:, LANES:]


def finish_outer(arrived_ref, x_ref, final_ref, copies_ref):
    total = x_ref[...].astype(F32)
    for i in range(arrived_ref.shape[0]):
        total += arrived_ref[i].astype(F32)
    scaled = (total * final_ref[...]).astype(BF)
    for i in range(copies_ref.shape[0]):
        copies_ref[i] = scaled


def attend(core_ref, mine_ref, other_ref, wk_ref, wv_ref, recip_ref, q_ref, g_ref, qg_ref, keep_ref, send_ref):
    core = core_ref[0]
    pairs = mine_ref.shape[0]
    rows = mine_ref.shape[1]
    scale = HEAD ** (-0.5)
    keys_raw = jnp.zeros((rows, HEAD), F32)
    values_raw = jnp.zeros((rows, HEAD), F32)
    square = jnp.zeros((rows, 1), F32)
    for z in range(pairs):
        for block_ref, side in ((mine_ref, core), (other_ref, 1 - core)):
            block = block_ref[z]
            keys_raw += dot(block, wk_ref[z, side])
            values_raw += dot(block, wv_ref[z, side])
            wide = block.astype(F32) * recip_ref[z, side]
            square += jnp.sum(wide * wide, axis=1, keepdims=True)
    inv_out = lax.rsqrt(square / D + EPSILON)
    keys = (keys_raw * inv_out).astype(BF)
    values = (values_raw * inv_out).astype(BF)
    key_grad = jnp.zeros((rows, HEAD), F32)
    value_grad = jnp.zeros((rows, HEAD), F32)
    step = 256
    for at in range(0, q_ref.shape[0], step):
        query = q_ref[at : at + step, :]
        grad = g_ref[at : at + step, :]
        scores = dot(keys, query, COLS) * scale
        raised = jnp.exp(scores - jnp.max(scores, axis=0, keepdims=True))
        probs = raised / jnp.sum(raised, axis=0, keepdims=True)
        probs_bf = probs.astype(BF)
        dprob = dot(values, grad, COLS)
        delta = jnp.sum(probs_bf.astype(F32) * dprob, axis=0, keepdims=True)
        dscore = (probs * (dprob - delta) * scale).astype(BF)
        qg_ref[at : at + step, :] = dot(dscore, keys, ROWS).astype(BF)
        key_grad += dot(dscore, query)
        value_grad += dot(probs_bf, grad)
    key_grad = key_grad.astype(BF)
    value_grad = value_grad.astype(BF)
    inner = jnp.sum(
        key_grad.astype(F32) * keys_raw + value_grad.astype(F32) * values_raw, axis=1, keepdims=True
    )
    along = inv_out * inv_out * inv_out * inner * (1.0 / D)
    for z in range(pairs):
        for block_ref, out_ref, side in ((mine_ref, keep_ref, core), (other_ref, send_ref, 1 - core)):
            total = dot(key_grad, wk_ref[z, side], COLS) + dot(value_grad, wv_ref[z, side], COLS)
            recip = recip_ref[z, side]
            term = inv_out * total - block_ref[z].astype(F32) * (recip * recip) * along
            out_ref[z] = term.astype(out_ref.dtype)


def outer_gradient(arrived_ref, final_ref, grad_ref, copies_ref):
    totals = [arrived_ref[i].astype(F32) for i in range(8)]
    for i in range(8, arrived_ref.shape[0]):
        totals[i % 8] += arrived_ref[i].astype(F32)
    total = sum(totals[1:], totals[0]) * final_ref[...]
    grad_ref[...] = total
    rounded = total.astype(BF)
    for i in range(copies_ref.shape[0]):
        copies_ref[i] = rounded


def through_down(core_ref, outer_ref, down_ref, got_ref, pieces_ref):
    core = core_ref[0]
    feats = down_ref.shape[1]
    half = down_ref.shape[0] // 2
    part = dot(outer_ref[core], down_ref[half_of(core, half), :], COLS)
    part += dot(outer_ref[1 - core], down_half(got_ref, feats, half), COLS)
    pieces_ref[...] = part.astype(BF).reshape(pieces_ref.shape)


def gate_up_gradient(arrived_ref, gate_f_ref, up_f_ref, inner_f_ref, copies_ref):
    half = gate_f_ref.shape[1]
    total = arrived_ref[0].astype(F32)
    for i in range(1, arrived_ref.shape[0]):
        total += arrived_ref[i].astype(F32)
    gate = (total * gate_f_ref[...]).astype(BF)
    up = (total * up_f_ref[...]).astype(BF)
    inner = in_two_lanes(jnp.sum(total * inner_f_ref[...], axis=1, keepdims=True))
    for i in range(copies_ref.shape[0]):
        copies_ref[i, :, :half] = gate
        copies_ref[i, :, half : 2 * half] = up
        copies_ref[i, :, 2 * half :] = inner


def through_gate_up(core_ref, grads_ref, x_ref, mlp_ref, gate_ref, up_ref, got_ref, pieces_ref):
    core = core_ref[0]
    half = gate_ref.shape[1] // 2
    feats = gate_ref.shape[0]
    here = half_of(core, half)
    tokens = x_ref.shape[1]
    shape = pieces_ref.shape[1:]
    gate = grads_ref[:, :, :half].reshape(tokens, half)
    up = grads_ref[:, :, half : 2 * half].reshape(tokens, half)
    inner = from_two_lanes(grads_ref[:, :, 2 * half :].astype(F32).reshape(tokens, LANES))
    part = dot(gate, gate_ref[:, here], COLS) + dot(up, up_ref[:, here], COLS)
    part = part * mlp_ref[...] - x_ref[core].astype(F32) * inner
    pieces_ref[core] = part.astype(BF).reshape(shape)
    mlp_there, _ = got_gains(got_ref, feats + half // 4)
    part = dot(gate, got_ref[:feats, :half], COLS) + dot(up, got_ref[:feats, half:], COLS)
    part = part * mlp_there - x_ref[1 - core].astype(F32) * inner
    pieces_ref[1 - core] = part.astype(BF).reshape(shape)


def gate_up_weights(core_ref, scaled_ref, here_ref, there_ref, gate_ref, up_ref):
    core = core_ref[0]
    half = gate_ref.shape[1] // 2
    tokens = scaled_ref.shape[0]
    scaled = scaled_ref[...]
    for grads_ref, place in ((here_ref, core), (there_ref, 1 - core)):
        at = half_of(place, half)
        gate_ref[:, at] = dot(scaled, grads_ref[:, :, :half].reshape(tokens, half), ROWS).astype(BF)
        up = grads_ref[:, :, half : 2 * half].reshape(tokens, half)
        up_ref[:, at] = dot(scaled, up, ROWS).astype(BF)


def down_weights(core_ref, outer_ref, here_ref, there_ref, down_ref):
    core = core_ref[0]
    half = down_ref.shape[0] // 2
    tokens = outer_ref.shape[1]
    share = here_ref.shape[1] - 16
    outer = outer_ref[core]
    for act_ref, place in ((here_ref, core), (there_ref, 1 - core)):
        act = act_ref[:, :share].reshape(tokens, half)
        down_ref[half_of(place, half), :] = dot(act, outer, ROWS).astype(BF)


def call(body, outs, *args, flops=0):
    vmem = pl.BlockSpec(memory_space=pltpu.VMEM)
    in_specs = [vmem] * len(args)
    if args[0].dtype == jnp.int32:
        in_specs[0] = pl.BlockSpec(memory_space=pltpu.SMEM)
    shapes = tuple(jax.ShapeDtypeStruct(shape, dtype) for shape, dtype in outs)
    moved = sum(a.size * a.dtype.itemsize for a in (*args, *shapes))
    results = pl.pallas_call(
        body,
        out_shape=shapes,
        in_specs=in_specs,
        out_specs=(vmem,) * len(shapes),
        compiler_params=pltpu.CompilerParams(vmem_limit_bytes=40 * 1024 * 1024),
        cost_estimate=pl.CostEstimate(flops=flops, bytes_accessed=moved, transcendentals=0),
    )(*args)
    return results


def on_device(
    enc_hidden,
    mlp_gain,
    final_gain,
    w_gate,
    w_up,
    w_down,
    key_weight,
    value_weight,
    queries,
    context_grad,
):
    block, feats = enc_hidden.shape
    half = w_gate.shape[1] // 2
    core = lax.axis_index("core").astype(jnp.int32).reshape(1)
    chips = lax.axis_size("z")
    blocks = lax.axis_size("tensor")
    tokens = block * blocks
    share = tokens // chips
    mlp_gain = mlp_gain.reshape(1, feats)
    final_gain = final_gain.reshape(1, feats)

    copies, sent = call(
        start,
        [((2 * blocks, block, feats), BF), ((feats + half // 4 + 16, 2 * half), BF)],
        core, enc_hidden, mlp_gain, final_gain, w_gate, w_up, w_down,
    )
    hidden = exchange(copies, WIDE).reshape(2, tokens, feats)
    got = other_core(sent)
    pieces, scaled = call(
        gate_up,
        [((chips, share, 2 * half + LANES), BF), ((tokens, feats), BF)],
        core, hidden, mlp_gain, w_gate, w_up, got,
    )
    arrived = exchange(pieces, "z")
    copies, gate_f, up_f, inner_f = call(
        activate,
        [((chips, share + 16, half), BF)] + [((share, half), F32)] * 3,
        core, arrived, final_gain, got,
    )
    act = exchange(copies, "z")
    act_there = other_core(act)
    pieces, recip = call(
        mix,
        [((2, blocks, block, feats), BF), ((chips, 2, 1, LANES), F32)],
        core, act, w_down, got,
    )
    arrived = exchange(pieces.reshape(-1, block, feats), WIDE)
    (copies,) = call(
        finish_outer, [((chips * blocks, block, feats), BF)], arrived, enc_hidden, final_gain
    )
    mine = exchange(copies, ("z", "tensor")).reshape(chips, tokens, feats)
    other = other_core(mine)
    by_block = (chips, 2, LANES, HEAD)
    query_grad, keep, send = call(
        attend,
        [(queries.shape[1:], BF), (mine.shape, F32), (mine.shape, BF)],
        core, mine, other, key_weight.reshape(by_block), value_weight.reshape(by_block), recip,
        queries[0], context_grad[0],
        flops=3_500_000_000,
    )
    both = (keep + other_core(send).astype(F32)).astype(BF)
    arrived = exchange(both.reshape(-1, block, feats), ("z", "tensor"))
    outer_grad, copies = call(
        outer_gradient,
        [((block, feats), F32), ((2 * blocks, block, feats), BF)],
        arrived, final_gain,
    )
    outer = exchange(copies, WIDE).reshape(2, tokens, feats)
    (pieces,) = call(through_down, [((chips, share, half), BF)], core, outer, w_down, got)
    arrived = exchange(pieces, "z")
    (down_weight_grad,) = call(down_weights, [(w_down.shape, BF)], core, outer, act, act_there)
    (copies,) = call(
        gate_up_gradient, [((chips, share, 2 * half + LANES), BF)], arrived, gate_f, up_f, inner_f
    )
    grads = exchange(copies, "z")
    grads_there = other_core(grads)
    (pieces,) = call(
        through_gate_up,
        [((2, blocks, block, feats), BF)],
        core, grads, hidden, mlp_gain, w_gate, w_up, got,
    )
    arrived = exchange(pieces.reshape(-1, block, feats), WIDE)
    gate_weight_grad, up_weight_grad = call(
        gate_up_weights,
        [(w_gate.shape, BF), (w_up.shape, BF)],
        core, scaled, grads, grads_there,
    )
    hidden_grad = outer_grad + arrived.astype(F32).sum(axis=0)
    return (query_grad[None], hidden_grad, gate_weight_grad, up_weight_grad, down_weight_grad)


def solution(mesh):
    names = list(mesh.axis_names)
    at = names.index("section")
    shape = list(mesh.devices.shape)
    names[at : at + 1] = SECTION
    shape[at : at + 1] = [shape[at] // 2, 2]
    fine = Mesh(mesh.devices.reshape(shape), tuple(names))
    in_specs = (
        P(("dp", "tensor"), SECTION),
        P(SECTION),
        P(SECTION),
        P(SECTION, "tensor"),
        P(SECTION, "tensor"),
        P("tensor", SECTION),
        P(SECTION, None, "tensor"),
        P(SECTION, None, "tensor"),
        P(SECTION, "dp", "tensor"),
        P(SECTION, "dp", "tensor"),
    )
    out_specs = (
        P(SECTION, "dp", "tensor"),
        P(("dp", "tensor"), SECTION),
        P(("dp", *SECTION), "tensor"),
        P(("dp", *SECTION), "tensor"),
        P(("dp", "tensor"), SECTION),
    )
    return jax.shard_map(
        on_device, mesh=fine, in_specs=in_specs, out_specs=out_specs, check_vma=False
    )
```

```python
import jax
import jax.numpy as jnp
from jax import lax
from jax.experimental import pallas as pl
from jax.experimental.pallas import tpu as pltpu
from jax.sharding import Mesh
from jax.sharding import PartitionSpec as P

D = 2048
HEAD = 256
LANES = 128
EPSILON = 1e-06
BF = jnp.bfloat16
F32 = jnp.float32

ROWS = (((0,), (0,)), ((), ()))
COLS = (((1,), (1,)), ((), ()))
SECTION = ("z", "core")
WIDE = ("core", "tensor")


def exchange(pieces, axis):
    return lax.all_to_all(pieces, axis, split_axis=0, concat_axis=0, tiled=True)


def other_core(value):
    return lax.ppermute(value, "core", [(0, 1), (1, 0)])


def dot(left, right, dims=(((1,), (0,)), ((), ()))):
    return lax.dot_general(left, right, dims, preferred_element_type=F32)


def in_thirds(value):
    high = value.astype(BF).astype(F32)
    middle = (value - high).astype(BF).astype(F32)
    return high, middle, value - high - middle


def diagonal(count, shift):
    row = lax.broadcasted_iota(jnp.int32, (count, LANES), 0)
    return row + shift == lax.broadcasted_iota(jnp.int32, (count, LANES), 1)


def as_column(line, count, shift=0):
    return jnp.sum(jnp.where(diagonal(count, shift), line, 0.0), axis=1, keepdims=True)


def in_blocks(value):
    width = value.shape[1]
    return jnp.concatenate([value[:, i : i + LANES] for i in range(0, width, LANES)], axis=0)


def half_of(core, half):
    return pl.ds(pl.multiple_of(core * half, half), half)


def spread(x_ref, copies_ref):
    for i in range(copies_ref.shape[0]):
        copies_ref[i] = x_ref[...]


def by_row(rows, count):
    row = lax.broadcasted_iota(jnp.int32, (count, LANES), 0)
    tile = jnp.zeros((count, LANES), F32)
    for i, value in enumerate(rows):
        tile = jnp.where(row == i, value, tile)
    return tile


def start(place_ref, mlp_ref, final_ref, gate_ref, up_ref, down_ref, sent_ref):
    half = gate_ref.shape[1] // 2
    feats = gate_ref.shape[0]
    quarter = half // 4
    away = 1 - lax.rem(place_ref[0], 2)
    there = half_of(away, half)
    sent_ref[:feats, :half] = gate_ref[:, there]
    sent_ref[:feats, half:] = up_ref[:, there]
    for i in range(4):
        at = pl.ds(pl.multiple_of(away * half + i * quarter, quarter), quarter)
        sent_ref[feats : feats + quarter, i * LANES : (i + 1) * LANES] = down_ref[at, :]
    for i, parts in enumerate(zip(in_thirds(mlp_ref[...]), in_thirds(final_ref[...]))):
        sent_ref[feats + quarter :, i * LANES : (i + 1) * LANES] = by_row(parts, 16).astype(BF)
    sent_ref[feats + quarter :, 3 * LANES :] = jnp.zeros((16, LANES), BF)


def got_gains(got_ref, rows):
    tile = got_ref[rows : rows + 16, :].astype(F32)
    tile = tile[:, :LANES] + tile[:, LANES : 2 * LANES] + tile[:, 2 * LANES : 3 * LANES]
    return tile[0:1], tile[1:2]


def gate_up(place_ref, x_ref, mlp_ref, final_ref, gate_ref, up_ref, got_ref, pieces_ref, scaled_ref):
    core = lax.rem(place_ref[0], 2)
    half = gate_ref.shape[1] // 2
    feats = gate_ref.shape[0]
    here = half_of(core, half)
    x_here = x_ref[core].astype(F32)
    x_there = x_ref[1 - core].astype(F32)
    scaled = (x_here * mlp_ref[...]).astype(BF)
    scaled_ref[...] = scaled
    mlp_there, final_there = got_gains(got_ref, feats + half // 4)
    scaled_there = (x_there * mlp_there).astype(BF)
    gate = dot(scaled, gate_ref[:, here]) + dot(scaled_there, got_ref[:feats, :half])
    up = dot(scaled, up_ref[:, here]) + dot(scaled_there, got_ref[:feats, half:])
    pieces = pieces_ref.shape[0]
    tokens = scaled.shape[0]
    share = tokens // pieces
    for at, value in ((0, gate), (half, up)):
        for lanes in range(0, half, LANES):
            rows = (at + lanes) // LANES * share
            part = value[:, lanes : lanes + LANES].astype(BF).reshape(pieces, share, LANES)
            pieces_ref[:, rows : rows + share, :] = part
    squares = x_here * x_here + x_there * x_there
    line = lax.dot_general(
        jnp.ones((8, LANES), F32),
        squares,
        COLS,
        precision=lax.Precision.HIGHEST,
        preferred_element_type=F32,
    )[0:1]
    high = line.astype(BF).astype(F32)
    first = core == 0
    final_here = final_ref[...]
    gains = in_thirds(jnp.where(first, final_here, final_there))
    gains += in_thirds(jnp.where(first, final_there, final_here))
    base = by_row(gains, 16)
    row = lax.broadcasted_iota(jnp.int32, (16, LANES), 0)
    for at in range(0, tokens, LANES):
        lanes = slice(at, at + LANES)
        tile = jnp.where(row == 6, high[:, lanes], base)
        tile = jnp.where(row == 7, (line - high)[:, lanes], tile).astype(BF)
        for i in range(at // share, (at + LANES) // share):
            pieces_ref[i, 2 * half // LANES * share :, :] = tile


def activate(place_ref, arrived_ref, copies_ref, gate_f_ref, up_f_ref, inner_f_ref, recip_ref):
    pieces, share, half = copies_ref.shape
    rows = 2 * half // LANES * share
    total = arrived_ref[0, :rows].astype(F32)
    for i in range(1, pieces):
        total += arrived_ref[i, :rows].astype(F32)
    line = jnp.zeros((1, LANES), F32)
    for i in range(pieces):
        tile = arrived_ref[i, rows:].astype(F32)
        recip_ref[i, 0] = 1.0 / (tile[0:1] + tile[1:2] + tile[2:3])
        recip_ref[i, 1] = 1.0 / (tile[3:4] + tile[4:5] + tile[5:6])
        line += tile[6:7] + tile[7:8]
    shift = lax.rem(lax.div(place_ref[0], 2), LANES // share) * share
    inv = lax.rsqrt(as_column(line, share, shift) * (1.0 / D) + EPSILON)
    parts = [total[i * share : (i + 1) * share] for i in range(2 * half // LANES)]
    gate_pre = jnp.concatenate(parts[: half // LANES], axis=1) * inv
    up_pre = jnp.concatenate(parts[half // LANES :], axis=1) * inv
    sigmoid_gate = jax.nn.sigmoid(gate_pre)
    activated = gate_pre * sigmoid_gate
    hidden_act = (activated * up_pre).astype(BF)
    gate_factor = up_pre * sigmoid_gate * (1.0 + gate_pre * (1.0 - sigmoid_gate))
    gate_f_ref[...] = gate_factor * inv
    up_f_ref[...] = activated * inv
    inner_f_ref[...] = (gate_factor * gate_pre + activated * up_pre) * (inv * inv * (1.0 / D))
    for i in range(pieces):
        copies_ref[i] = hidden_act


def down_half(got_ref, feats, half):
    quarter = half // 4
    rows = got_ref[feats : feats + quarter, :]
    return jnp.concatenate([rows[:, i * LANES : (i + 1) * LANES] for i in range(4)], axis=0)


def mix(place_ref, act_ref, down_ref, got_ref, pieces_ref):
    core = lax.rem(place_ref[0], 2)
    pieces, share, half = act_ref.shape
    feats = down_ref.shape[1]
    act = act_ref[...].reshape(pieces * share, half)
    shape = pieces_ref.shape[1:]
    here = dot(act, down_ref[half_of(core, half), :])
    pieces_ref[core] = here.astype(BF).reshape(shape)
    there = dot(act, down_half(got_ref, feats, half))
    pieces_ref[1 - core] = there.astype(BF).reshape(shape)


def finish_outer(arrived_ref, x_ref, final_ref, copies_ref):
    total = x_ref[...].astype(F32)
    for i in range(arrived_ref.shape[0]):
        total += arrived_ref[i].astype(F32)
    scaled = (total * final_ref[...]).astype(BF)
    for i in range(copies_ref.shape[0]):
        copies_ref[i] = scaled


def attend(place_ref, mine_ref, other_ref, wk_ref, wv_ref, recip_ref, q_ref, g_ref, qg_ref, keep_ref, send_ref):
    core = lax.rem(place_ref[0], 2)
    pairs = mine_ref.shape[0]
    rows = mine_ref.shape[1]
    scale = HEAD ** (-0.5)
    keys_raw = jnp.zeros((rows, HEAD), F32)
    values_raw = jnp.zeros((rows, HEAD), F32)
    square = jnp.zeros((rows, LANES), F32)

    def both_sides(ref, z):
        return jnp.concatenate([ref[z, core], ref[z, 1 - core]], axis=0)

    for z in range(pairs):
        block = jnp.concatenate([mine_ref[z], other_ref[z]], axis=1)
        keys_raw += dot(block, both_sides(wk_ref, z))
        values_raw += dot(block, both_sides(wv_ref, z))
        for block_ref, side in ((mine_ref, core), (other_ref, 1 - core)):
            wide = block_ref[z].astype(F32) * recip_ref[z, side]
            square += wide * wide
    inv_out = lax.rsqrt(jnp.sum(square, axis=1, keepdims=True) / D + EPSILON)
    keys = (keys_raw * inv_out).astype(BF)
    values = (values_raw * inv_out).astype(BF)
    key_grad = jnp.zeros((rows, HEAD), F32)
    value_grad = jnp.zeros((rows, HEAD), F32)
    step = 256
    for at in range(0, q_ref.shape[0], step):
        query = q_ref[at : at + step, :]
        grad = g_ref[at : at + step, :]
        scores = dot(keys, query, COLS) * scale
        raised = jnp.exp(scores - jnp.max(scores, axis=0, keepdims=True))
        probs = raised / jnp.sum(raised, axis=0, keepdims=True)
        probs_bf = probs.astype(BF)
        dprob = dot(values, grad, COLS)
        delta = jnp.sum(probs_bf.astype(F32) * dprob, axis=0, keepdims=True)
        dscore = (probs * (dprob - delta) * scale).astype(BF)
        qg_ref[at : at + step, :] = dot(dscore, keys, ROWS).astype(BF)
        key_grad += dot(dscore, query)
        value_grad += dot(probs_bf, grad)
    key_grad = key_grad.astype(BF)
    value_grad = value_grad.astype(BF)
    inner = jnp.sum(
        key_grad.astype(F32) * keys_raw + value_grad.astype(F32) * values_raw, axis=1, keepdims=True
    )
    along = inv_out * inv_out * inv_out * inner * (1.0 / D)
    for z in range(pairs):
        total = dot(key_grad, both_sides(wk_ref, z), COLS)
        total += dot(value_grad, both_sides(wv_ref, z), COLS)
        total *= inv_out
        sides = ((mine_ref, keep_ref, core), (other_ref, send_ref, 1 - core))
        for i, (block_ref, out_ref, side) in enumerate(sides):
            recip = recip_ref[z, side]
            term = block_ref[z].astype(F32) * (recip * recip) * along
            out_ref[z] = (total[:, i * LANES : (i + 1) * LANES] - term).astype(out_ref.dtype)


def outer_gradient(arrived_ref, final_ref, grad_ref, copies_ref):
    totals = [arrived_ref[i].astype(F32) for i in range(8)]
    for i in range(8, arrived_ref.shape[0]):
        totals[i % 8] += arrived_ref[i].astype(F32)
    total = sum(totals[1:], totals[0]) * final_ref[...]
    grad_ref[...] = total
    rounded = total.astype(BF)
    for i in range(copies_ref.shape[0]):
        copies_ref[i] = rounded


def through_down(place_ref, outer_ref, down_ref, got_ref, pieces_ref):
    core = lax.rem(place_ref[0], 2)
    feats = down_ref.shape[1]
    half = down_ref.shape[0] // 2
    part = dot(outer_ref[core], down_ref[half_of(core, half), :], COLS)
    part += dot(outer_ref[1 - core], down_half(got_ref, feats, half), COLS)
    pieces_ref[...] = part.astype(BF).reshape(pieces_ref.shape)


def gate_up_gradient(arrived_ref, gate_f_ref, up_f_ref, inner_f_ref, copies_ref):
    half = gate_f_ref.shape[1]
    total = arrived_ref[0].astype(F32)
    for i in range(1, arrived_ref.shape[0]):
        total += arrived_ref[i].astype(F32)
    gate = in_blocks((total * gate_f_ref[...]).astype(BF))
    up = in_blocks((total * up_f_ref[...]).astype(BF))
    inner = jnp.sum(total * inner_f_ref[...], axis=1, keepdims=True)
    line = jnp.sum(jnp.where(diagonal(inner.shape[0], 0), inner, 0.0), axis=0, keepdims=True)
    high = line.astype(BF).astype(F32)
    tile = by_row((high, line - high), 16).astype(BF)
    rows = gate.shape[0]
    for i in range(copies_ref.shape[0]):
        copies_ref[i, :rows] = gate
        copies_ref[i, rows : 2 * rows] = up
        copies_ref[i, 2 * rows :] = tile


def columns_of(grads_ref, at, half):
    share = (grads_ref.shape[1] - 16) * LANES // (2 * half)
    blocks = range(at // LANES, (at + half) // LANES)
    tokens = grads_ref.shape[0] * share
    parts = [grads_ref[:, i * share : (i + 1) * share].reshape(tokens, LANES) for i in blocks]
    return jnp.concatenate(parts, axis=1)


def through_gate_up(place_ref, grads_ref, x_ref, mlp_ref, gate_ref, up_ref, got_ref, pieces_ref):
    core = lax.rem(place_ref[0], 2)
    half = gate_ref.shape[1] // 2
    feats = gate_ref.shape[0]
    here = half_of(core, half)
    tokens = x_ref.shape[1]
    shape = pieces_ref.shape[1:]
    gate = columns_of(grads_ref, 0, half)
    up = columns_of(grads_ref, half, half)
    share = tokens // grads_ref.shape[0]
    lines = [grads_ref[i, grads_ref.shape[1] - 16 :].astype(F32) for i in range(grads_ref.shape[0])]
    inner = jnp.concatenate([as_column(v[0:1] + v[1:2], share) for v in lines], axis=0)
    part = dot(gate, gate_ref[:, here], COLS) + dot(up, up_ref[:, here], COLS)
    part = part * mlp_ref[...] - x_ref[core].astype(F32) * inner
    pieces_ref[core] = part.astype(BF).reshape(shape)
    mlp_there, _ = got_gains(got_ref, feats + half // 4)
    part = dot(gate, got_ref[:feats, :half], COLS) + dot(up, got_ref[:feats, half:], COLS)
    part = part * mlp_there - x_ref[1 - core].astype(F32) * inner
    pieces_ref[1 - core] = part.astype(BF).reshape(shape)


def gate_up_weights(place_ref, scaled_ref, here_ref, there_ref, gate_ref, up_ref):
    core = lax.rem(place_ref[0], 2)
    half = gate_ref.shape[1] // 2
    scaled = scaled_ref[...]
    for grads_ref, place in ((here_ref, core), (there_ref, 1 - core)):
        at = half_of(place, half)
        gate_ref[:, at] = dot(scaled, columns_of(grads_ref, 0, half), ROWS).astype(BF)
        up_ref[:, at] = dot(scaled, columns_of(grads_ref, half, half), ROWS).astype(BF)


def down_weights(place_ref, outer_ref, here_ref, there_ref, down_ref):
    core = lax.rem(place_ref[0], 2)
    half = down_ref.shape[0] // 2
    tokens = outer_ref.shape[1]
    outer = outer_ref[core]
    for act_ref, place in ((here_ref, core), (there_ref, 1 - core)):
        act = act_ref[...].reshape(tokens, half)
        down_ref[half_of(place, half), :] = dot(act, outer, ROWS).astype(BF)


def call(body, outs, *args, flops=0):
    vmem = pl.BlockSpec(memory_space=pltpu.VMEM)
    in_specs = [vmem] * len(args)
    if args[0].dtype == jnp.int32:
        in_specs[0] = pl.BlockSpec(memory_space=pltpu.SMEM)
    shapes = tuple(jax.ShapeDtypeStruct(shape, dtype) for shape, dtype in outs)
    moved = sum(a.size * a.dtype.itemsize for a in (*args, *shapes))
    results = pl.pallas_call(
        body,
        out_shape=shapes,
        in_specs=in_specs,
        out_specs=(vmem,) * len(shapes),
        compiler_params=pltpu.CompilerParams(vmem_limit_bytes=40 * 1024 * 1024),
        cost_estimate=pl.CostEstimate(flops=flops, bytes_accessed=moved, transcendentals=0),
    )(*args)
    return results


def on_device(
    enc_hidden,
    mlp_gain,
    final_gain,
    w_gate,
    w_up,
    w_down,
    key_weight,
    value_weight,
    queries,
    context_grad,
):
    block, feats = enc_hidden.shape
    half = w_gate.shape[1] // 2
    place = (2 * lax.axis_index("z") + lax.axis_index("core")).astype(jnp.int32).reshape(1)
    chips = lax.axis_size("z")
    blocks = lax.axis_size("tensor")
    tokens = block * blocks
    share = tokens // chips
    mlp_gain = mlp_gain.reshape(1, feats)
    final_gain = final_gain.reshape(1, feats)

    piece = share * 2 * half // LANES + 16

    (copies,) = call(spread, [((2 * blocks, block, feats), BF)], enc_hidden)
    hidden = exchange(copies, WIDE).reshape(2, tokens, feats)
    (sent,) = call(
        start,
        [((feats + half // 4 + 16, 2 * half), BF)],
        place, mlp_gain, final_gain, w_gate, w_up, w_down,
    )
    got = other_core(sent)
    pieces, scaled = call(
        gate_up,
        [((chips, piece, LANES), BF), ((tokens, feats), BF)],
        place, hidden, mlp_gain, final_gain, w_gate, w_up, got,
    )
    arrived = exchange(pieces, "z")
    copies, gate_f, up_f, inner_f, recip = call(
        activate,
        [((chips, share, half), BF)]
        + [((share, half), F32)] * 3
        + [((chips, 2, 1, LANES), F32)],
        place, arrived,
    )
    act = exchange(copies, "z")
    act_there = other_core(act)
    (pieces,) = call(
        mix, [((2, blocks, block, feats), BF)], place, act, w_down, got
    )
    arrived = exchange(pieces.reshape(-1, block, feats), WIDE)
    (copies,) = call(
        finish_outer, [((chips * blocks, block, feats), BF)], arrived, enc_hidden, final_gain
    )
    mine = exchange(copies, ("z", "tensor")).reshape(chips, tokens, feats)
    other = other_core(mine)
    by_block = (chips, 2, LANES, HEAD)
    query_grad, keep, send = call(
        attend,
        [(queries.shape[1:], BF), (mine.shape, F32), (mine.shape, BF)],
        place, mine, other, key_weight.reshape(by_block), value_weight.reshape(by_block), recip,
        queries[0], context_grad[0],
        flops=3_500_000_000,
    )
    both = (keep + other_core(send).astype(F32)).astype(BF)
    arrived = exchange(both.reshape(-1, block, feats), ("z", "tensor"))
    outer_grad, copies = call(
        outer_gradient,
        [((block, feats), F32), ((2 * blocks, block, feats), BF)],
        arrived, final_gain,
    )
    outer = exchange(copies, WIDE).reshape(2, tokens, feats)
    (pieces,) = call(through_down, [((chips, share, half), BF)], place, outer, w_down, got)
    arrived = exchange(pieces, "z")
    (down_weight_grad,) = call(down_weights, [(w_down.shape, BF)], place, outer, act, act_there)
    (copies,) = call(
        gate_up_gradient, [((chips, piece, LANES), BF)], arrived, gate_f, up_f, inner_f
    )
    grads = exchange(copies, "z")
    grads_there = other_core(grads)
    (pieces,) = call(
        through_gate_up,
        [((2, blocks, block, feats), BF)],
        place, grads, hidden, mlp_gain, w_gate, w_up, got,
    )
    arrived = exchange(pieces.reshape(-1, block, feats), WIDE)
    gate_weight_grad, up_weight_grad = call(
        gate_up_weights,
        [(w_gate.shape, BF), (w_up.shape, BF)],
        place, scaled, grads, grads_there,
    )
    outer_grad, gate_weight_grad, up_weight_grad = lax.optimization_barrier(
        (outer_grad, gate_weight_grad, up_weight_grad)
    )
    hidden_grad = outer_grad + arrived.astype(F32).sum(axis=0)
    return (query_grad[None], hidden_grad, gate_weight_grad, up_weight_grad, down_weight_grad)


def solution(mesh):
    names = list(mesh.axis_names)
    at = names.index("section")
    shape = list(mesh.devices.shape)
    names[at : at + 1] = SECTION
    shape[at : at + 1] = [shape[at] // 2, 2]
    fine = Mesh(mesh.devices.reshape(shape), tuple(names))
    in_specs = (
        P(("dp", "tensor"), SECTION),
        P(SECTION),
        P(SECTION),
        P(SECTION, "tensor"),
        P(SECTION, "tensor"),
        P("tensor", SECTION),
        P(SECTION, None, "tensor"),
        P(SECTION, None, "tensor"),
        P(SECTION, "dp", "tensor"),
        P(SECTION, "dp", "tensor"),
    )
    out_specs = (
        P(SECTION, "dp", "tensor"),
        P(("dp", "tensor"), SECTION),
        P(("dp", *SECTION), "tensor"),
        P(("dp", *SECTION), "tensor"),
        P(("dp", "tensor"), SECTION),
    )
    return jax.shard_map(
        on_device, mesh=fine, in_specs=in_specs, out_specs=out_specs, check_vma=False
    )
```

```python
import jax
import jax.numpy as jnp
from jax import lax
from jax.experimental import pallas as pl
from jax.experimental.pallas import tpu as pltpu
from jax.sharding import Mesh
from jax.sharding import PartitionSpec as P

D = 2048
HEAD = 256
LANES = 128
EPSILON = 1e-06
BF = jnp.bfloat16
F32 = jnp.float32

ROWS = (((0,), (0,)), ((), ()))
COLS = (((1,), (1,)), ((), ()))
SECTION = ("z", "core")
WIDE = ("core", "tensor")


def exchange(pieces, axis):
    return lax.all_to_all(pieces, axis, split_axis=0, concat_axis=0, tiled=True)


def other_core(value):
    return lax.ppermute(value, "core", [(0, 1), (1, 0)])


def dot(left, right, dims=(((1,), (0,)), ((), ()))):
    return lax.dot_general(left, right, dims, preferred_element_type=F32)


def in_thirds(value):
    high = value.astype(BF).astype(F32)
    middle = (value - high).astype(BF).astype(F32)
    return high, middle, value - high - middle


def diagonal(count, shift):
    row = lax.broadcasted_iota(jnp.int32, (count, LANES), 0)
    return row + shift == lax.broadcasted_iota(jnp.int32, (count, LANES), 1)


def as_column(line, count, shift=0):
    return jnp.sum(jnp.where(diagonal(count, shift), line, 0.0), axis=1, keepdims=True)


def in_blocks(value):
    width = value.shape[1]
    return jnp.concatenate([value[:, i : i + LANES] for i in range(0, width, LANES)], axis=0)


def half_of(core, half):
    return pl.ds(pl.multiple_of(core * half, half), half)


def spread(x_ref, copies_ref):
    for i in range(copies_ref.shape[0]):
        copies_ref[i] = x_ref[...]


def by_row(rows, count):
    row = lax.broadcasted_iota(jnp.int32, (count, LANES), 0)
    tile = jnp.zeros((count, LANES), F32)
    for i, value in enumerate(rows):
        tile = jnp.where(row == i, value, tile)
    return tile


def start(place_ref, mlp_ref, final_ref, gate_ref, up_ref, down_ref, sent_ref):
    half = gate_ref.shape[1] // 2
    feats = gate_ref.shape[0]
    quarter = half // 4
    away = 1 - lax.rem(place_ref[0], 2)
    there = half_of(away, half)
    sent_ref[:feats, :half] = gate_ref[:, there]
    sent_ref[:feats, half:] = up_ref[:, there]
    for i in range(4):
        at = pl.ds(pl.multiple_of(away * half + i * quarter, quarter), quarter)
        sent_ref[feats : feats + quarter, i * LANES : (i + 1) * LANES] = down_ref[at, :]
    for i, parts in enumerate(zip(in_thirds(mlp_ref[...]), in_thirds(final_ref[...]))):
        sent_ref[feats + quarter :, i * LANES : (i + 1) * LANES] = by_row(parts, 16).astype(BF)
    sent_ref[feats + quarter :, 3 * LANES :] = jnp.zeros((16, LANES), BF)


def got_gains(got_ref, rows):
    tile = got_ref[rows : rows + 16, :].astype(F32)
    tile = tile[:, :LANES] + tile[:, LANES : 2 * LANES] + tile[:, 2 * LANES : 3 * LANES]
    return tile[0:1], tile[1:2]


def gate_up(place_ref, x_ref, mlp_ref, final_ref, gate_ref, up_ref, got_ref, pieces_ref, scaled_ref):
    core = lax.rem(place_ref[0], 2)
    half = gate_ref.shape[1] // 2
    feats = gate_ref.shape[0]
    here = half_of(core, half)
    x_here = x_ref[core].astype(F32)
    x_there = x_ref[1 - core].astype(F32)
    scaled = (x_here * mlp_ref[...]).astype(BF)
    scaled_ref[...] = scaled
    mlp_there, final_there = got_gains(got_ref, feats + half // 4)
    scaled_there = (x_there * mlp_there).astype(BF)
    both = jnp.concatenate([scaled, scaled_there], axis=1)
    weights = jnp.concatenate([gate_ref[:, here], up_ref[:, here]], axis=1)
    weights = jnp.concatenate([weights, got_ref[:feats, :]], axis=0)
    gate_and_up = dot(both, weights).astype(BF)
    pieces = pieces_ref.shape[0]
    tokens = scaled.shape[0]
    share = tokens // pieces
    for i in range(2 * half // LANES):
        part = gate_and_up[:, i * LANES : (i + 1) * LANES].reshape(pieces, share, LANES)
        pieces_ref[:, i * share : (i + 1) * share, :] = part
    squares = x_here * x_here + x_there * x_there
    line = lax.dot_general(
        jnp.ones((8, LANES), F32),
        squares,
        COLS,
        precision=lax.Precision.HIGHEST,
        preferred_element_type=F32,
    )[0:1]
    high = line.astype(BF).astype(F32)
    first = core == 0
    final_here = final_ref[...]
    gains = in_thirds(jnp.where(first, final_here, final_there))
    gains += in_thirds(jnp.where(first, final_there, final_here))
    base = by_row(gains, 16)
    row = lax.broadcasted_iota(jnp.int32, (16, LANES), 0)
    for at in range(0, tokens, LANES):
        lanes = slice(at, at + LANES)
        tile = jnp.where(row == 6, high[:, lanes], base)
        tile = jnp.where(row == 7, (line - high)[:, lanes], tile).astype(BF)
        for i in range(at // share, (at + LANES) // share):
            pieces_ref[i, 2 * half // LANES * share :, :] = tile


def activate(place_ref, arrived_ref, copies_ref, gate_f_ref, up_f_ref, inner_f_ref, recip_ref):
    pieces, share, half = copies_ref.shape
    rows = 2 * half // LANES * share
    total = arrived_ref[0, :rows].astype(F32)
    for i in range(1, pieces):
        total += arrived_ref[i, :rows].astype(F32)
    line = jnp.zeros((1, LANES), F32)
    for i in range(pieces):
        tile = arrived_ref[i, rows:].astype(F32)
        recip_ref[i, 0] = 1.0 / (tile[0:1] + tile[1:2] + tile[2:3])
        recip_ref[i, 1] = 1.0 / (tile[3:4] + tile[4:5] + tile[5:6])
        line += tile[6:7] + tile[7:8]
    shift = lax.rem(lax.div(place_ref[0], 2), LANES // share) * share
    inv = lax.rsqrt(as_column(line, share, shift) * (1.0 / D) + EPSILON)
    parts = [total[i * share : (i + 1) * share] for i in range(2 * half // LANES)]
    gate_pre = jnp.concatenate(parts[: half // LANES], axis=1) * inv
    up_pre = jnp.concatenate(parts[half // LANES :], axis=1) * inv
    sigmoid_gate = jax.nn.sigmoid(gate_pre)
    activated = gate_pre * sigmoid_gate
    hidden_act = (activated * up_pre).astype(BF)
    gate_factor = up_pre * sigmoid_gate * (1.0 + gate_pre * (1.0 - sigmoid_gate))
    gate_f_ref[...] = gate_factor * inv
    up_f_ref[...] = activated * inv
    inner_f_ref[...] = (gate_factor * gate_pre + activated * up_pre) * (inv * inv * (1.0 / D))
    for i in range(pieces):
        copies_ref[i] = hidden_act


def down_half(got_ref, feats, half):
    quarter = half // 4
    rows = got_ref[feats : feats + quarter, :]
    return jnp.concatenate([rows[:, i * LANES : (i + 1) * LANES] for i in range(4)], axis=0)


def both_downs(core, down_ref, got_ref):
    feats = down_ref.shape[1]
    half = down_ref.shape[0] // 2
    here = down_ref[half_of(core, half), :]
    return jnp.concatenate([here, down_half(got_ref, feats, half)], axis=1)


def mix(place_ref, act_ref, down_ref, got_ref, pieces_ref):
    core = lax.rem(place_ref[0], 2)
    pieces, share, half = act_ref.shape
    feats = down_ref.shape[1]
    act = act_ref[...].reshape(pieces * share, half)
    shape = pieces_ref.shape[1:]
    mixed = dot(act, both_downs(core, down_ref, got_ref)).astype(BF)
    pieces_ref[core] = mixed[:, :feats].reshape(shape)
    pieces_ref[1 - core] = mixed[:, feats:].reshape(shape)


def finish_outer(arrived_ref, x_ref, final_ref, copies_ref):
    total = x_ref[...].astype(F32)
    for i in range(arrived_ref.shape[0]):
        total += arrived_ref[i].astype(F32)
    scaled = (total * final_ref[...]).astype(BF)
    for i in range(copies_ref.shape[0]):
        copies_ref[i] = scaled


def two_blocks(ref, z, side):
    return jnp.concatenate([ref[z, side], ref[z + 1, side]], axis=0)


def add_features(block_ref, side, wk_ref, wv_ref, recip_ref, keys, values, square):
    for z in range(0, block_ref.shape[0], 2):
        block = jnp.concatenate([block_ref[z], block_ref[z + 1]], axis=1)
        keys += dot(block, two_blocks(wk_ref, z, side))
        values += dot(block, two_blocks(wv_ref, z, side))
        for i in range(2):
            wide = block_ref[z + i].astype(F32) * recip_ref[z + i, side]
            square += wide * wide
    return keys, values, square


def project(place_ref, mine_ref, wk_ref, wv_ref, recip_ref, keys_ref, values_ref, square_ref):
    core = lax.rem(place_ref[0], 2)
    keys_ref[...], values_ref[...], square_ref[...] = add_features(
        mine_ref,
        core,
        wk_ref,
        wv_ref,
        recip_ref,
        jnp.zeros(keys_ref.shape, F32),
        jnp.zeros(values_ref.shape, F32),
        jnp.zeros(square_ref.shape, F32),
    )


def back_to_features(block_ref, side, wk_ref, wv_ref, recip_ref, grads, scales, out_ref):
    key_grad, value_grad = grads
    inv_out, along = scales
    for z in range(0, block_ref.shape[0], 2):
        total = dot(key_grad, two_blocks(wk_ref, z, side), COLS)
        total += dot(value_grad, two_blocks(wv_ref, z, side), COLS)
        for i in range(2):
            recip = recip_ref[z + i, side]
            term = block_ref[z + i].astype(F32) * (recip * recip) * along
            part = total[:, i * LANES : (i + 1) * LANES] * inv_out - term
            out_ref[z + i] = part.astype(out_ref.dtype)


def attend(place_ref, other_ref, wk_ref, wv_ref, recip_ref, keys_ref, values_ref, square_ref, q_ref, g_ref, *outs):
    qg_ref, send_ref, grads_ref, scales_ref = outs
    core = lax.rem(place_ref[0], 2)
    rows = other_ref.shape[1]
    scale = HEAD ** (-0.5)
    keys_raw, values_raw, square = add_features(
        other_ref,
        1 - core,
        wk_ref,
        wv_ref,
        recip_ref,
        keys_ref[...],
        values_ref[...],
        square_ref[...],
    )
    inv_out = lax.rsqrt(jnp.sum(square, axis=1, keepdims=True) / D + EPSILON)
    keys = (keys_raw * inv_out).astype(BF)
    values = (values_raw * inv_out).astype(BF)
    scaled_keys = (keys.astype(F32) * scale).astype(BF)
    scaled_values = (values.astype(F32) * scale).astype(BF)
    key_grad = jnp.zeros((rows, HEAD), F32)
    value_grad = jnp.zeros((rows, HEAD), F32)
    step = 256
    for at in range(0, q_ref.shape[0], step):
        query = q_ref[at : at + step, :]
        grad = g_ref[at : at + step, :]
        scores = dot(scaled_keys, query, COLS)
        raised = jnp.exp(scores - jnp.max(scores, axis=0, keepdims=True))
        probs = raised * (1.0 / jnp.sum(raised, axis=0, keepdims=True))
        probs_bf = probs.astype(BF)
        dprob = dot(scaled_values, grad, COLS)
        delta = jnp.sum(probs_bf.astype(F32) * dprob, axis=0, keepdims=True)
        dscore = (probs * (dprob - delta)).astype(BF)
        qg_ref[at : at + step, :] = dot(dscore, keys, ROWS).astype(BF)
        key_grad += dot(dscore, query)
        value_grad += dot(probs_bf, grad)
    key_grad = key_grad.astype(BF)
    value_grad = value_grad.astype(BF)
    inner = jnp.sum(
        key_grad.astype(F32) * keys_raw + value_grad.astype(F32) * values_raw, axis=1, keepdims=True
    )
    along = inv_out * inv_out * inv_out * inner * (1.0 / D)
    grads_ref[0] = key_grad
    grads_ref[1] = value_grad
    scales_ref[0] = jnp.broadcast_to(inv_out, (rows, LANES))
    scales_ref[1] = jnp.broadcast_to(along, (rows, LANES))
    grads = (key_grad, value_grad)
    scales = (inv_out, along)
    back_to_features(other_ref, 1 - core, wk_ref, wv_ref, recip_ref, grads, scales, send_ref)


def keep_own(place_ref, mine_ref, wk_ref, wv_ref, recip_ref, grads_ref, scales_ref, keep_ref):
    core = lax.rem(place_ref[0], 2)
    grads = (grads_ref[0], grads_ref[1])
    scales = (scales_ref[0], scales_ref[1])
    back_to_features(mine_ref, core, wk_ref, wv_ref, recip_ref, grads, scales, keep_ref)


def outer_gradient(arrived_ref, final_ref, grad_ref, copies_ref):
    totals = [arrived_ref[i].astype(F32) for i in range(8)]
    for i in range(8, arrived_ref.shape[0]):
        totals[i % 8] += arrived_ref[i].astype(F32)
    total = sum(totals[1:], totals[0]) * final_ref[...]
    grad_ref[...] = total
    rounded = total.astype(BF)
    for i in range(copies_ref.shape[0]):
        copies_ref[i] = rounded


def through_down(place_ref, outer_ref, down_ref, got_ref, pieces_ref):
    core = lax.rem(place_ref[0], 2)
    outer = jnp.concatenate([outer_ref[core], outer_ref[1 - core]], axis=1)
    part = dot(outer, both_downs(core, down_ref, got_ref), COLS)
    pieces_ref[...] = part.astype(BF).reshape(pieces_ref.shape)


def gate_up_gradient(arrived_ref, gate_f_ref, up_f_ref, inner_f_ref, copies_ref):
    half = gate_f_ref.shape[1]
    total = arrived_ref[0].astype(F32)
    for i in range(1, arrived_ref.shape[0]):
        total += arrived_ref[i].astype(F32)
    gate = in_blocks((total * gate_f_ref[...]).astype(BF))
    up = in_blocks((total * up_f_ref[...]).astype(BF))
    inner = jnp.sum(total * inner_f_ref[...], axis=1, keepdims=True)
    line = jnp.sum(jnp.where(diagonal(inner.shape[0], 0), inner, 0.0), axis=0, keepdims=True)
    high = line.astype(BF).astype(F32)
    tile = by_row((high, line - high), 16).astype(BF)
    rows = gate.shape[0]
    for i in range(copies_ref.shape[0]):
        copies_ref[i, :rows] = gate
        copies_ref[i, rows : 2 * rows] = up
        copies_ref[i, 2 * rows :] = tile


def columns_of(grads_ref, at, width, whole):
    share = (grads_ref.shape[1] - 16) * LANES // whole
    blocks = range(at // LANES, (at + width) // LANES)
    tokens = grads_ref.shape[0] * share
    parts = [grads_ref[:, i * share : (i + 1) * share].reshape(tokens, LANES) for i in blocks]
    return jnp.concatenate(parts, axis=1)


def through_gate_up(place_ref, grads_ref, x_ref, mlp_ref, gate_ref, up_ref, got_ref, pieces_ref):
    core = lax.rem(place_ref[0], 2)
    half = gate_ref.shape[1] // 2
    feats = gate_ref.shape[0]
    here = half_of(core, half)
    tokens = x_ref.shape[1]
    shape = pieces_ref.shape[1:]
    weights = jnp.concatenate([gate_ref[:, here], up_ref[:, here]], axis=1)
    weights = jnp.concatenate([weights, got_ref[:feats, :]], axis=0)
    total = dot(columns_of(grads_ref, 0, 2 * half, 2 * half), weights, COLS)
    share = tokens // grads_ref.shape[0]
    lines = [grads_ref[i, grads_ref.shape[1] - 16 :].astype(F32) for i in range(grads_ref.shape[0])]
    inner = jnp.concatenate([as_column(v[0:1] + v[1:2], share) for v in lines], axis=0)
    part = total[:, :feats] * mlp_ref[...] - x_ref[core].astype(F32) * inner
    pieces_ref[core] = part.astype(BF).reshape(shape)
    mlp_there, _ = got_gains(got_ref, feats + half // 4)
    part = total[:, feats:] * mlp_there - x_ref[1 - core].astype(F32) * inner
    pieces_ref[1 - core] = part.astype(BF).reshape(shape)


def finish(place_ref, scaled_ref, here_ref, there_ref, normed_ref, outer_ref, gate_ref, up_ref, grad_ref):
    core = lax.rem(place_ref[0], 2)
    half = gate_ref.shape[1] // 2
    scaled = scaled_ref[...]
    for grads_ref, place in ((here_ref, core), (there_ref, 1 - core)):
        at = half_of(place, half)
        both = dot(scaled, columns_of(grads_ref, 0, 2 * half, 2 * half), ROWS).astype(BF)
        gate_ref[:, at] = both[:, :half]
        up_ref[:, at] = both[:, half:]
    grad_ref[...] = outer_ref[...] + normed_ref[...]


def down_weights(place_ref, outer_ref, here_ref, there_ref, down_ref):
    core = lax.rem(place_ref[0], 2)
    half = down_ref.shape[0] // 2
    tokens = outer_ref.shape[1]
    outer = outer_ref[core]
    for act_ref, place in ((here_ref, core), (there_ref, 1 - core)):
        act = act_ref[...].reshape(tokens, half)
        down_ref[half_of(place, half), :] = dot(act, outer, ROWS).astype(BF)


def call(body, outs, *args, flops=0):
    vmem = pl.BlockSpec(memory_space=pltpu.VMEM)
    in_specs = [vmem] * len(args)
    if args[0].dtype == jnp.int32:
        in_specs[0] = pl.BlockSpec(memory_space=pltpu.SMEM)
    shapes = tuple(jax.ShapeDtypeStruct(shape, dtype) for shape, dtype in outs)
    moved = sum(a.size * a.dtype.itemsize for a in (*args, *shapes))
    results = pl.pallas_call(
        body,
        out_shape=shapes,
        in_specs=in_specs,
        out_specs=(vmem,) * len(shapes),
        compiler_params=pltpu.CompilerParams(vmem_limit_bytes=40 * 1024 * 1024),
        cost_estimate=pl.CostEstimate(flops=flops, bytes_accessed=moved, transcendentals=0),
    )(*args)
    return results


def on_device(
    enc_hidden,
    mlp_gain,
    final_gain,
    w_gate,
    w_up,
    w_down,
    key_weight,
    value_weight,
    queries,
    context_grad,
):
    block, feats = enc_hidden.shape
    half = w_gate.shape[1] // 2
    place = (2 * lax.axis_index("z") + lax.axis_index("core")).astype(jnp.int32).reshape(1)
    chips = lax.axis_size("z")
    blocks = lax.axis_size("tensor")
    tokens = block * blocks
    share = tokens // chips
    mlp_gain = mlp_gain.reshape(1, feats)
    final_gain = final_gain.reshape(1, feats)

    piece = share * 2 * half // LANES + 16

    (copies,) = call(spread, [((2 * blocks, block, feats), BF)], enc_hidden)
    hidden = exchange(copies, WIDE).reshape(2, tokens, feats)
    (sent,) = call(
        start,
        [((feats + half // 4 + 16, 2 * half), BF)],
        place, mlp_gain, final_gain, w_gate, w_up, w_down,
    )
    got = other_core(sent)
    pieces, scaled = call(
        gate_up,
        [((chips, piece, LANES), BF), ((tokens, feats), BF)],
        place, hidden, mlp_gain, final_gain, w_gate, w_up, got,
    )
    arrived = exchange(pieces, "z")
    copies, gate_f, up_f, inner_f, recip = call(
        activate,
        [((chips, share, half), BF)]
        + [((share, half), F32)] * 3
        + [((chips, 2, 1, LANES), F32)],
        place, arrived,
    )
    act = exchange(copies, "z")
    act_there = other_core(act)
    (pieces,) = call(
        mix, [((2, blocks, block, feats), BF)], place, act, w_down, got
    )
    arrived = exchange(pieces.reshape(-1, block, feats), WIDE)
    (copies,) = call(
        finish_outer, [((chips * blocks, block, feats), BF)], arrived, enc_hidden, final_gain
    )
    mine = exchange(copies, ("z", "tensor")).reshape(chips, tokens, feats)
    other = other_core(mine)
    by_block = (chips, 2, LANES, HEAD)
    weights = (key_weight.reshape(by_block), value_weight.reshape(by_block), recip)
    projected = call(
        project,
        [((tokens, HEAD), F32)] * 2 + [((tokens, LANES), F32)],
        place, mine, *weights,
        flops=270_000_000,
    )
    query_grad, send, layer_grads, scales = call(
        attend,
        [
            (queries.shape[1:], BF),
            (mine.shape, BF),
            ((2, tokens, HEAD), BF),
            ((2, tokens, LANES), F32),
        ],
        place, other, *weights, *projected, queries[0], context_grad[0],
        flops=1_200_000_000,
    )
    (keep,) = call(
        keep_own, [(mine.shape, F32)], place, mine, *weights, layer_grads, scales, flops=270_000_000
    )
    both = (keep + other_core(send).astype(F32)).astype(BF)
    arrived = exchange(both.reshape(-1, block, feats), ("z", "tensor"))
    outer_grad, copies = call(
        outer_gradient,
        [((block, feats), F32), ((2 * blocks, block, feats), BF)],
        arrived, final_gain,
    )
    outer = exchange(copies, WIDE).reshape(2, tokens, feats)
    (pieces,) = call(through_down, [((chips, share, half), BF)], place, outer, w_down, got)
    arrived = exchange(pieces, "z")
    (down_weight_grad,) = call(down_weights, [(w_down.shape, BF)], place, outer, act, act_there)
    (copies,) = call(
        gate_up_gradient, [((chips, piece, LANES), BF)], arrived, gate_f, up_f, inner_f
    )
    grads = exchange(copies, "z")
    grads_there = other_core(grads)
    (pieces,) = call(
        through_gate_up,
        [((2, blocks, block, feats), BF)],
        place, grads, hidden, mlp_gain, w_gate, w_up, got,
    )
    arrived = exchange(pieces.reshape(-1, block, feats), WIDE)
    gate_weight_grad, up_weight_grad, hidden_grad = call(
        finish,
        [(w_gate.shape, BF), (w_up.shape, BF), ((block, feats), F32)],
        place, scaled, grads, grads_there, arrived.astype(F32).sum(axis=0), outer_grad,
    )
    return (query_grad[None], hidden_grad, gate_weight_grad, up_weight_grad, down_weight_grad)


def solution(mesh):
    names = list(mesh.axis_names)
    at = names.index("section")
    shape = list(mesh.devices.shape)
    names[at : at + 1] = SECTION
    shape[at : at + 1] = [shape[at] // 2, 2]
    fine = Mesh(mesh.devices.reshape(shape), tuple(names))
    in_specs = (
        P(("dp", "tensor"), SECTION),
        P(SECTION),
        P(SECTION),
        P(SECTION, "tensor"),
        P(SECTION, "tensor"),
        P("tensor", SECTION),
        P(SECTION, None, "tensor"),
        P(SECTION, None, "tensor"),
        P(SECTION, "dp", "tensor"),
        P(SECTION, "dp", "tensor"),
    )
    out_specs = (
        P(SECTION, "dp", "tensor"),
        P(("dp", "tensor"), SECTION),
        P(("dp", *SECTION), "tensor"),
        P(("dp", *SECTION), "tensor"),
        P(("dp", "tensor"), SECTION),
    )
    return jax.shard_map(
        on_device, mesh=fine, in_specs=in_specs, out_specs=out_specs, check_vma=False
    )
```

```python
import jax
import jax.numpy as jnp
from jax import lax
from jax.experimental import pallas as pl
from jax.experimental.pallas import tpu as pltpu
from jax.sharding import Mesh
from jax.sharding import PartitionSpec as P

D = 2048
HEAD = 256
LANES = 128
EPSILON = 1e-06
BF = jnp.bfloat16
F32 = jnp.float32

ROWS = (((0,), (0,)), ((), ()))
COLS = (((1,), (1,)), ((), ()))
SECTION = ("z", "core")
WIDE = ("core", "tensor")


def exchange(pieces, axis):
    return lax.all_to_all(pieces, axis, split_axis=0, concat_axis=0, tiled=True)


def other_core(value):
    return lax.ppermute(value, "core", [(0, 1), (1, 0)])


def dot(left, right, dims=(((1,), (0,)), ((), ()))):
    return lax.dot_general(left, right, dims, preferred_element_type=F32)


def in_thirds(value):
    high = value.astype(BF).astype(F32)
    middle = (value - high).astype(BF).astype(F32)
    return high, middle, value - high - middle


def diagonal(count, shift):
    row = lax.broadcasted_iota(jnp.int32, (count, LANES), 0)
    return row + shift == lax.broadcasted_iota(jnp.int32, (count, LANES), 1)


def as_column(line, count, shift=0):
    return jnp.sum(jnp.where(diagonal(count, shift), line, 0.0), axis=1, keepdims=True)


def in_blocks(value):
    width = value.shape[1]
    return jnp.concatenate([value[:, i : i + LANES] for i in range(0, width, LANES)], axis=0)


def half_of(core, half):
    return pl.ds(pl.multiple_of(core * half, half), half)


def spread(x_ref, copies_ref):
    for i in range(copies_ref.shape[0]):
        copies_ref[i] = x_ref[...]


def by_row(rows, count):
    row = lax.broadcasted_iota(jnp.int32, (count, LANES), 0)
    tile = jnp.zeros((count, LANES), F32)
    for i, value in enumerate(rows):
        tile = jnp.where(row == i, value, tile)
    return tile


def start(place_ref, mlp_ref, final_ref, gate_ref, up_ref, down_ref, sent_ref):
    half = gate_ref.shape[1] // 2
    feats = gate_ref.shape[0]
    quarter = half // 4
    away = 1 - lax.rem(place_ref[0], 2)
    there = half_of(away, half)
    sent_ref[:feats, :half] = gate_ref[:, there]
    sent_ref[:feats, half:] = up_ref[:, there]
    for i in range(4):
        at = pl.ds(pl.multiple_of(away * half + i * quarter, quarter), quarter)
        sent_ref[feats : feats + quarter, i * LANES : (i + 1) * LANES] = down_ref[at, :]
    for i, parts in enumerate(zip(in_thirds(mlp_ref[...]), in_thirds(final_ref[...]))):
        sent_ref[feats + quarter :, i * LANES : (i + 1) * LANES] = by_row(parts, 16).astype(BF)
    sent_ref[feats + quarter :, 3 * LANES :] = jnp.zeros((16, LANES), BF)


def got_gains(got_ref, rows):
    tile = got_ref[rows : rows + 16, :].astype(F32)
    tile = tile[:, :LANES] + tile[:, LANES : 2 * LANES] + tile[:, 2 * LANES : 3 * LANES]
    return tile[0:1], tile[1:2]


def gate_up(place_ref, x_ref, mlp_ref, final_ref, gate_ref, up_ref, got_ref, pieces_ref, scaled_ref):
    core = lax.rem(place_ref[0], 2)
    half = gate_ref.shape[1] // 2
    feats = gate_ref.shape[0]
    here = half_of(core, half)
    x_here = x_ref[core].astype(F32)
    x_there = x_ref[1 - core].astype(F32)
    scaled = (x_here * mlp_ref[...]).astype(BF)
    scaled_ref[...] = scaled
    mlp_there, final_there = got_gains(got_ref, feats + half // 4)
    scaled_there = (x_there * mlp_there).astype(BF)
    both = jnp.concatenate([scaled, scaled_there], axis=1)
    weights = jnp.concatenate([gate_ref[:, here], up_ref[:, here]], axis=1)
    weights = jnp.concatenate([weights, got_ref[:feats, :]], axis=0)
    gate_and_up = dot(both, weights).astype(BF)
    pieces = pieces_ref.shape[0]
    tokens = scaled.shape[0]
    share = tokens // pieces
    for i in range(2 * half // LANES):
        part = gate_and_up[:, i * LANES : (i + 1) * LANES].reshape(pieces, share, LANES)
        pieces_ref[:, i * share : (i + 1) * share, :] = part
    squares = x_here * x_here + x_there * x_there
    line = lax.dot_general(
        jnp.ones((8, LANES), F32),
        squares,
        COLS,
        precision=lax.Precision.HIGHEST,
        preferred_element_type=F32,
    )[0:1]
    high = line.astype(BF).astype(F32)
    first = core == 0
    final_here = final_ref[...]
    gains = in_thirds(jnp.where(first, final_here, final_there))
    gains += in_thirds(jnp.where(first, final_there, final_here))
    base = by_row(gains, 16)
    row = lax.broadcasted_iota(jnp.int32, (16, LANES), 0)
    for at in range(0, tokens, LANES):
        lanes = slice(at, at + LANES)
        tile = jnp.where(row == 6, high[:, lanes], base)
        tile = jnp.where(row == 7, (line - high)[:, lanes], tile).astype(BF)
        for i in range(at // share, (at + LANES) // share):
            pieces_ref[i, 2 * half // LANES * share :, :] = tile


def activate(place_ref, arrived_ref, copies_ref, gate_f_ref, up_f_ref, inner_f_ref, recip_ref):
    pieces, share, half = copies_ref.shape
    rows = 2 * half // LANES * share
    total = arrived_ref[0, :rows].astype(F32)
    for i in range(1, pieces):
        total += arrived_ref[i, :rows].astype(F32)
    line = jnp.zeros((1, LANES), F32)
    for i in range(pieces):
        tile = arrived_ref[i, rows:].astype(F32)
        recip_ref[i, 0] = 1.0 / (tile[0:1] + tile[1:2] + tile[2:3])
        recip_ref[i, 1] = 1.0 / (tile[3:4] + tile[4:5] + tile[5:6])
        line += tile[6:7] + tile[7:8]
    shift = lax.rem(lax.div(place_ref[0], 2), LANES // share) * share
    inv = lax.rsqrt(as_column(line, share, shift) * (1.0 / D) + EPSILON)
    parts = [total[i * share : (i + 1) * share] for i in range(2 * half // LANES)]
    gate_pre = jnp.concatenate(parts[: half // LANES], axis=1) * inv
    up_pre = jnp.concatenate(parts[half // LANES :], axis=1) * inv
    sigmoid_gate = jax.nn.sigmoid(gate_pre)
    activated = gate_pre * sigmoid_gate
    hidden_act = (activated * up_pre).astype(BF)
    gate_factor = up_pre * sigmoid_gate * (1.0 + gate_pre * (1.0 - sigmoid_gate))
    gate_f_ref[...] = gate_factor * inv
    up_f_ref[...] = activated * inv
    inner_f_ref[...] = (gate_factor * gate_pre + activated * up_pre) * (inv * inv * (1.0 / D))
    for i in range(pieces):
        copies_ref[i] = hidden_act


def down_half(got_ref, feats, half):
    quarter = half // 4
    rows = got_ref[feats : feats + quarter, :]
    return jnp.concatenate([rows[:, i * LANES : (i + 1) * LANES] for i in range(4)], axis=0)


def both_downs(core, down_ref, got_ref):
    feats = down_ref.shape[1]
    half = down_ref.shape[0] // 2
    here = down_ref[half_of(core, half), :]
    return jnp.concatenate([here, down_half(got_ref, feats, half)], axis=1)


def mix(place_ref, act_ref, down_ref, got_ref, pieces_ref):
    core = lax.rem(place_ref[0], 2)
    pieces, share, half = act_ref.shape
    feats = down_ref.shape[1]
    act = act_ref[...].reshape(pieces * share, half)
    shape = pieces_ref.shape[1:]
    mixed = dot(act, both_downs(core, down_ref, got_ref)).astype(BF)
    pieces_ref[core] = mixed[:, :feats].reshape(shape)
    pieces_ref[1 - core] = mixed[:, feats:].reshape(shape)


def finish_outer(arrived_ref, x_ref, final_ref, copies_ref):
    total = x_ref[...].astype(F32)
    for i in range(arrived_ref.shape[0]):
        total += arrived_ref[i].astype(F32)
    scaled = (total * final_ref[...]).astype(BF)
    for i in range(copies_ref.shape[0]):
        copies_ref[i] = scaled


def two_blocks(ref, z, side):
    return jnp.concatenate([ref[z, side], ref[z + 1, side]], axis=0)


def add_features(block_ref, side, wk_ref, wv_ref, recip_ref, keys, values, square):
    for z in range(0, block_ref.shape[0], 2):
        block = jnp.concatenate([block_ref[z], block_ref[z + 1]], axis=1)
        keys += dot(block, two_blocks(wk_ref, z, side))
        values += dot(block, two_blocks(wv_ref, z, side))
        for i in range(2):
            wide = block_ref[z + i].astype(F32) * recip_ref[z + i, side]
            square += wide * wide
    return keys, values, square


def project(place_ref, mine_ref, wk_ref, wv_ref, recip_ref, keys_ref, values_ref, square_ref):
    core = lax.rem(place_ref[0], 2)
    keys_ref[...], values_ref[...], square_ref[...] = add_features(
        mine_ref,
        core,
        wk_ref,
        wv_ref,
        recip_ref,
        jnp.zeros(keys_ref.shape, F32),
        jnp.zeros(values_ref.shape, F32),
        jnp.zeros(square_ref.shape, F32),
    )


def back_to_features(block_ref, side, wk_ref, wv_ref, recip_ref, grads, scales, out_ref):
    key_grad, value_grad = grads
    inv_out, along = scales
    for z in range(0, block_ref.shape[0], 2):
        total = dot(key_grad, two_blocks(wk_ref, z, side), COLS)
        total += dot(value_grad, two_blocks(wv_ref, z, side), COLS)
        for i in range(2):
            recip = recip_ref[z + i, side]
            term = block_ref[z + i].astype(F32) * (recip * recip) * along
            part = total[:, i * LANES : (i + 1) * LANES] * inv_out - term
            out_ref[z + i] = part.astype(out_ref.dtype)


def attend(place_ref, other_ref, wk_ref, wv_ref, recip_ref, keys_ref, values_ref, square_ref, q_ref, g_ref, *outs):
    qg_ref, send_ref, grads_ref, scales_ref, held_ref, sems = outs
    core = lax.rem(place_ref[0], 2)
    rows = other_ref.shape[1]
    scale = HEAD ** (-0.5)
    keys_raw, values_raw, square = add_features(
        other_ref,
        1 - core,
        wk_ref,
        wv_ref,
        recip_ref,
        keys_ref[...],
        values_ref[...],
        square_ref[...],
    )
    inv_out = lax.rsqrt(jnp.sum(square, axis=1, keepdims=True) / D + EPSILON)
    keys = (keys_raw * inv_out).astype(BF)
    values = (values_raw * inv_out).astype(BF)
    scaled_keys = (keys.astype(F32) * scale).astype(BF)
    scaled_values = (values.astype(F32) * scale).astype(BF)
    key_grad = jnp.zeros((rows, HEAD), F32)
    value_grad = jnp.zeros((rows, HEAD), F32)
    step = 256
    leaving = []
    for at in range(0, q_ref.shape[0], step):
        query = q_ref[at : at + step, :]
        grad = g_ref[at : at + step, :]
        scores = dot(scaled_keys, query, COLS)
        raised = jnp.exp(scores - jnp.max(scores, axis=0, keepdims=True))
        probs = raised * (1.0 / jnp.sum(raised, axis=0, keepdims=True))
        probs_bf = probs.astype(BF)
        dprob = dot(scaled_values, grad, COLS)
        delta = jnp.sum(probs_bf.astype(F32) * dprob, axis=0, keepdims=True)
        dscore = (probs * (dprob - delta)).astype(BF)
        part = pl.ds(at, step)
        held_ref[part, :] = dot(dscore, keys, ROWS).astype(BF)
        leaving.append(
            pltpu.make_async_copy(held_ref.at[part, :], qg_ref.at[part, :], sems.at[at // step])
        )
        leaving[-1].start()
        key_grad += dot(dscore, query)
        value_grad += dot(probs_bf, grad)
    key_grad = key_grad.astype(BF)
    value_grad = value_grad.astype(BF)
    inner = jnp.sum(
        key_grad.astype(F32) * keys_raw + value_grad.astype(F32) * values_raw, axis=1, keepdims=True
    )
    along = inv_out * inv_out * inv_out * inner * (1.0 / D)
    grads_ref[0] = key_grad
    grads_ref[1] = value_grad
    scales_ref[0] = jnp.broadcast_to(inv_out, (rows, LANES))
    scales_ref[1] = jnp.broadcast_to(along, (rows, LANES))
    grads = (key_grad, value_grad)
    scales = (inv_out, along)
    back_to_features(other_ref, 1 - core, wk_ref, wv_ref, recip_ref, grads, scales, send_ref)
    for copy in leaving:
        copy.wait()


def keep_own(place_ref, mine_ref, wk_ref, wv_ref, recip_ref, grads_ref, scales_ref, keep_ref):
    core = lax.rem(place_ref[0], 2)
    grads = (grads_ref[0], grads_ref[1])
    scales = (scales_ref[0], scales_ref[1])
    back_to_features(mine_ref, core, wk_ref, wv_ref, recip_ref, grads, scales, keep_ref)


def outer_gradient(arrived_ref, final_ref, grad_ref, copies_ref):
    totals = [arrived_ref[i].astype(F32) for i in range(8)]
    for i in range(8, arrived_ref.shape[0]):
        totals[i % 8] += arrived_ref[i].astype(F32)
    total = sum(totals[1:], totals[0]) * final_ref[...]
    grad_ref[...] = total
    rounded = total.astype(BF)
    for i in range(copies_ref.shape[0]):
        copies_ref[i] = rounded


def through_down(place_ref, outer_ref, down_ref, got_ref, pieces_ref):
    core = lax.rem(place_ref[0], 2)
    outer = jnp.concatenate([outer_ref[core], outer_ref[1 - core]], axis=1)
    part = dot(outer, both_downs(core, down_ref, got_ref), COLS)
    pieces_ref[...] = part.astype(BF).reshape(pieces_ref.shape)


def gate_up_gradient(arrived_ref, gate_f_ref, up_f_ref, inner_f_ref, copies_ref):
    half = gate_f_ref.shape[1]
    total = arrived_ref[0].astype(F32)
    for i in range(1, arrived_ref.shape[0]):
        total += arrived_ref[i].astype(F32)
    gate = in_blocks((total * gate_f_ref[...]).astype(BF))
    up = in_blocks((total * up_f_ref[...]).astype(BF))
    inner = jnp.sum(total * inner_f_ref[...], axis=1, keepdims=True)
    line = jnp.sum(jnp.where(diagonal(inner.shape[0], 0), inner, 0.0), axis=0, keepdims=True)
    high = line.astype(BF).astype(F32)
    tile = by_row((high, line - high), 16).astype(BF)
    rows = gate.shape[0]
    for i in range(copies_ref.shape[0]):
        copies_ref[i, :rows] = gate
        copies_ref[i, rows : 2 * rows] = up
        copies_ref[i, 2 * rows :] = tile


def columns_of(grads_ref, at, width, whole):
    share = (grads_ref.shape[1] - 16) * LANES // whole
    blocks = range(at // LANES, (at + width) // LANES)
    tokens = grads_ref.shape[0] * share
    parts = [grads_ref[:, i * share : (i + 1) * share].reshape(tokens, LANES) for i in blocks]
    return jnp.concatenate(parts, axis=1)


def through_gate_up(place_ref, grads_ref, x_ref, mlp_ref, gate_ref, up_ref, got_ref, pieces_ref):
    core = lax.rem(place_ref[0], 2)
    half = gate_ref.shape[1] // 2
    feats = gate_ref.shape[0]
    here = half_of(core, half)
    tokens = x_ref.shape[1]
    shape = pieces_ref.shape[1:]
    weights = jnp.concatenate([gate_ref[:, here], up_ref[:, here]], axis=1)
    weights = jnp.concatenate([weights, got_ref[:feats, :]], axis=0)
    total = dot(columns_of(grads_ref, 0, 2 * half, 2 * half), weights, COLS)
    share = tokens // grads_ref.shape[0]
    lines = [grads_ref[i, grads_ref.shape[1] - 16 :].astype(F32) for i in range(grads_ref.shape[0])]
    inner = jnp.concatenate([as_column(v[0:1] + v[1:2], share) for v in lines], axis=0)
    part = total[:, :feats] * mlp_ref[...] - x_ref[core].astype(F32) * inner
    pieces_ref[core] = part.astype(BF).reshape(shape)
    mlp_there, _ = got_gains(got_ref, feats + half // 4)
    part = total[:, feats:] * mlp_there - x_ref[1 - core].astype(F32) * inner
    pieces_ref[1 - core] = part.astype(BF).reshape(shape)


def finish(place_ref, scaled_ref, here_ref, there_ref, normed_ref, outer_ref, gate_ref, up_ref, grad_ref):
    core = lax.rem(place_ref[0], 2)
    half = gate_ref.shape[1] // 2
    scaled = scaled_ref[...]
    for grads_ref, place in ((here_ref, core), (there_ref, 1 - core)):
        at = half_of(place, half)
        both = dot(scaled, columns_of(grads_ref, 0, 2 * half, 2 * half), ROWS).astype(BF)
        gate_ref[:, at] = both[:, :half]
        up_ref[:, at] = both[:, half:]
    grad_ref[...] = outer_ref[...] + normed_ref[...]


def down_weights(place_ref, outer_ref, here_ref, there_ref, down_ref):
    core = lax.rem(place_ref[0], 2)
    half = down_ref.shape[0] // 2
    tokens = outer_ref.shape[1]
    outer = outer_ref[core]
    for act_ref, place in ((here_ref, core), (there_ref, 1 - core)):
        act = act_ref[...].reshape(tokens, half)
        down_ref[half_of(place, half), :] = dot(act, outer, ROWS).astype(BF)


def call(body, outs, *args, flops=0, first_out=None, scratch=()):
    vmem = pl.BlockSpec(memory_space=pltpu.VMEM)
    in_specs = [vmem] * len(args)
    if args[0].dtype == jnp.int32:
        in_specs[0] = pl.BlockSpec(memory_space=pltpu.SMEM)
    shapes = tuple(jax.ShapeDtypeStruct(shape, dtype) for shape, dtype in outs)
    moved = sum(a.size * a.dtype.itemsize for a in (*args, *shapes))
    results = pl.pallas_call(
        body,
        out_shape=shapes,
        in_specs=in_specs,
        out_specs=(first_out or vmem,) + (vmem,) * (len(shapes) - 1),
        scratch_shapes=scratch,
        compiler_params=pltpu.CompilerParams(vmem_limit_bytes=40 * 1024 * 1024),
        cost_estimate=pl.CostEstimate(flops=flops, bytes_accessed=moved, transcendentals=0),
    )(*args)
    return results


def on_device(
    enc_hidden,
    mlp_gain,
    final_gain,
    w_gate,
    w_up,
    w_down,
    key_weight,
    value_weight,
    queries,
    context_grad,
):
    block, feats = enc_hidden.shape
    half = w_gate.shape[1] // 2
    place = (2 * lax.axis_index("z") + lax.axis_index("core")).astype(jnp.int32).reshape(1)
    chips = lax.axis_size("z")
    blocks = lax.axis_size("tensor")
    tokens = block * blocks
    share = tokens // chips
    mlp_gain = mlp_gain.reshape(1, feats)
    final_gain = final_gain.reshape(1, feats)

    piece = share * 2 * half // LANES + 16

    (copies,) = call(spread, [((2 * blocks, block, feats), BF)], enc_hidden)
    hidden = exchange(copies, WIDE).reshape(2, tokens, feats)
    (sent,) = call(
        start,
        [((feats + half // 4 + 16, 2 * half), BF)],
        place, mlp_gain, final_gain, w_gate, w_up, w_down,
    )
    got = other_core(sent)
    pieces, scaled = call(
        gate_up,
        [((chips, piece, LANES), BF), ((tokens, feats), BF)],
        place, hidden, mlp_gain, final_gain, w_gate, w_up, got,
    )
    arrived = exchange(pieces, "z")
    copies, gate_f, up_f, inner_f, recip = call(
        activate,
        [((chips, share, half), BF)]
        + [((share, half), F32)] * 3
        + [((chips, 2, 1, LANES), F32)],
        place, arrived,
    )
    act = exchange(copies, "z")
    act_there = other_core(act)
    (pieces,) = call(
        mix, [((2, blocks, block, feats), BF)], place, act, w_down, got
    )
    arrived = exchange(pieces.reshape(-1, block, feats), WIDE)
    (copies,) = call(
        finish_outer, [((chips * blocks, block, feats), BF)], arrived, enc_hidden, final_gain
    )
    mine = exchange(copies, ("z", "tensor")).reshape(chips, tokens, feats)
    other = other_core(mine)
    by_block = (chips, 2, LANES, HEAD)
    weights = (key_weight.reshape(by_block), value_weight.reshape(by_block), recip)
    projected = call(
        project,
        [((tokens, HEAD), F32)] * 2 + [((tokens, LANES), F32)],
        place, mine, *weights,
        flops=270_000_000,
    )
    query_grad, send, layer_grads, scales = call(
        attend,
        [
            (queries.shape[1:], BF),
            (mine.shape, BF),
            ((2, tokens, HEAD), BF),
            ((2, tokens, LANES), F32),
        ],
        place, other, *weights, *projected, queries[0], context_grad[0],
        flops=1_200_000_000,
        first_out=pl.BlockSpec(memory_space=pl.ANY),
        scratch=[pltpu.VMEM(queries.shape[1:], BF), pltpu.SemaphoreType.DMA((4,))],
    )
    (keep,) = call(
        keep_own, [(mine.shape, F32)], place, mine, *weights, layer_grads, scales, flops=270_000_000
    )
    both = (keep + other_core(send).astype(F32)).astype(BF)
    arrived = exchange(both.reshape(-1, block, feats), ("z", "tensor"))
    outer_grad, copies = call(
        outer_gradient,
        [((block, feats), F32), ((2 * blocks, block, feats), BF)],
        arrived, final_gain,
    )
    outer = exchange(copies, WIDE).reshape(2, tokens, feats)
    (pieces,) = call(through_down, [((chips, share, half), BF)], place, outer, w_down, got)
    arrived = exchange(pieces, "z")
    (down_weight_grad,) = call(down_weights, [(w_down.shape, BF)], place, outer, act, act_there)
    (copies,) = call(
        gate_up_gradient, [((chips, piece, LANES), BF)], arrived, gate_f, up_f, inner_f
    )
    grads = exchange(copies, "z")
    grads_there = other_core(grads)
    (pieces,) = call(
        through_gate_up,
        [((2, blocks, block, feats), BF)],
        place, grads, hidden, mlp_gain, w_gate, w_up, got,
    )
    arrived = exchange(pieces.reshape(-1, block, feats), WIDE)
    gate_weight_grad, up_weight_grad, hidden_grad = call(
        finish,
        [(w_gate.shape, BF), (w_up.shape, BF), ((block, feats), F32)],
        place, scaled, grads, grads_there, arrived.astype(F32).sum(axis=0), outer_grad,
    )
    return (query_grad[None], hidden_grad, gate_weight_grad, up_weight_grad, down_weight_grad)


def solution(mesh):
    names = list(mesh.axis_names)
    at = names.index("section")
    shape = list(mesh.devices.shape)
    names[at : at + 1] = SECTION
    shape[at : at + 1] = [shape[at] // 2, 2]
    fine = Mesh(mesh.devices.reshape(shape), tuple(names))
    in_specs = (
        P(("dp", "tensor"), SECTION),
        P(SECTION),
        P(SECTION),
        P(SECTION, "tensor"),
        P(SECTION, "tensor"),
        P("tensor", SECTION),
        P(SECTION, None, "tensor"),
        P(SECTION, None, "tensor"),
        P(SECTION, "dp", "tensor"),
        P(SECTION, "dp", "tensor"),
    )
    out_specs = (
        P(SECTION, "dp", "tensor"),
        P(("dp", "tensor"), SECTION),
        P(("dp", *SECTION), "tensor"),
        P(("dp", *SECTION), "tensor"),
        P(("dp", "tensor"), SECTION),
    )
    return jax.shard_map(
        on_device, mesh=fine, in_specs=in_specs, out_specs=out_specs, check_vma=False
    )
```

```python
import jax
import jax.numpy as jnp
from jax import lax
from jax.experimental import pallas as pl
from jax.experimental.pallas import tpu as pltpu
from jax.sharding import Mesh
from jax.sharding import PartitionSpec as P

D = 2048
HEAD = 256
LANES = 128
EPSILON = 1e-06
BF = jnp.bfloat16
F32 = jnp.float32

ROWS = (((0,), (0,)), ((), ()))
COLS = (((1,), (1,)), ((), ()))
SECTION = ("z", "core")
WIDE = ("core", "tensor")


def exchange(pieces, axis):
    return lax.all_to_all(pieces, axis, split_axis=0, concat_axis=0, tiled=True)


def other_core(value):
    return lax.ppermute(value, "core", [(0, 1), (1, 0)])


def dot(left, right, dims=(((1,), (0,)), ((), ()))):
    return lax.dot_general(left, right, dims, preferred_element_type=F32)


def in_thirds(value):
    high = value.astype(BF).astype(F32)
    middle = (value - high).astype(BF).astype(F32)
    return high, middle, value - high - middle


def diagonal(count, shift):
    row = lax.broadcasted_iota(jnp.int32, (count, LANES), 0)
    return row + shift == lax.broadcasted_iota(jnp.int32, (count, LANES), 1)


def as_column(line, count, shift=0):
    return jnp.sum(jnp.where(diagonal(count, shift), line, 0.0), axis=1, keepdims=True)


def in_blocks(value):
    width = value.shape[1]
    return jnp.concatenate([value[:, i : i + LANES] for i in range(0, width, LANES)], axis=0)


def half_of(core, half):
    return pl.ds(pl.multiple_of(core * half, half), half)


def spread(x_ref, copies_ref):
    for i in range(copies_ref.shape[0]):
        copies_ref[i] = x_ref[...]


def by_row(rows, count):
    row = lax.broadcasted_iota(jnp.int32, (count, LANES), 0)
    tile = jnp.zeros((count, LANES), F32)
    for i, value in enumerate(rows):
        tile = jnp.where(row == i, value, tile)
    return tile


def start(place_ref, mlp_ref, final_ref, gate_ref, up_ref, down_ref, sent_ref):
    half = gate_ref.shape[1] // 2
    feats = gate_ref.shape[0]
    quarter = half // 4
    away = 1 - lax.rem(place_ref[0], 2)
    there = half_of(away, half)
    sent_ref[:feats, :half] = gate_ref[:, there]
    sent_ref[:feats, half:] = up_ref[:, there]
    for i in range(4):
        at = pl.ds(pl.multiple_of(away * half + i * quarter, quarter), quarter)
        sent_ref[feats : feats + quarter, i * LANES : (i + 1) * LANES] = down_ref[at, :]
    for i, parts in enumerate(zip(in_thirds(mlp_ref[...]), in_thirds(final_ref[...]))):
        sent_ref[feats + quarter :, i * LANES : (i + 1) * LANES] = by_row(parts, 16).astype(BF)
    sent_ref[feats + quarter :, 3 * LANES :] = jnp.zeros((16, LANES), BF)


def got_gains(got_ref, rows):
    tile = got_ref[rows : rows + 16, :].astype(F32)
    tile = tile[:, :LANES] + tile[:, LANES : 2 * LANES] + tile[:, 2 * LANES : 3 * LANES]
    return tile[0:1], tile[1:2]


def gate_up(place_ref, x_ref, mlp_ref, final_ref, gate_ref, up_ref, got_ref, pieces_ref, scaled_ref):
    core = lax.rem(place_ref[0], 2)
    half = gate_ref.shape[1] // 2
    feats = gate_ref.shape[0]
    here = half_of(core, half)
    x_here = x_ref[core].astype(F32)
    x_there = x_ref[1 - core].astype(F32)
    scaled = (x_here * mlp_ref[...]).astype(BF)
    scaled_ref[...] = scaled
    mlp_there, final_there = got_gains(got_ref, feats + half // 4)
    scaled_there = (x_there * mlp_there).astype(BF)
    both = jnp.concatenate([scaled, scaled_there], axis=1)
    weights = jnp.concatenate([gate_ref[:, here], up_ref[:, here]], axis=1)
    weights = jnp.concatenate([weights, got_ref[:feats, :]], axis=0)
    gate_and_up = dot(both, weights).astype(BF)
    pieces = pieces_ref.shape[0]
    tokens = scaled.shape[0]
    share = tokens // pieces
    for i in range(2 * half // LANES):
        part = gate_and_up[:, i * LANES : (i + 1) * LANES].reshape(pieces, share, LANES)
        pieces_ref[:, i * share : (i + 1) * share, :] = part
    squares = x_here * x_here + x_there * x_there
    line = lax.dot_general(
        jnp.ones((8, LANES), F32),
        squares,
        COLS,
        precision=lax.Precision.HIGHEST,
        preferred_element_type=F32,
    )[0:1]
    high = line.astype(BF).astype(F32)
    first = core == 0
    final_here = final_ref[...]
    gains = in_thirds(jnp.where(first, final_here, final_there))
    gains += in_thirds(jnp.where(first, final_there, final_here))
    base = by_row(gains, 16)
    row = lax.broadcasted_iota(jnp.int32, (16, LANES), 0)
    for at in range(0, tokens, LANES):
        lanes = slice(at, at + LANES)
        tile = jnp.where(row == 6, high[:, lanes], base)
        tile = jnp.where(row == 7, (line - high)[:, lanes], tile).astype(BF)
        for i in range(at // share, (at + LANES) // share):
            pieces_ref[i, 2 * half // LANES * share :, :] = tile


def activate(place_ref, arrived_ref, copies_ref, gate_f_ref, up_f_ref, inner_f_ref, recip_ref):
    pieces, share, half = copies_ref.shape
    rows = 2 * half // LANES * share
    total = arrived_ref[0, :rows].astype(F32)
    for i in range(1, pieces):
        total += arrived_ref[i, :rows].astype(F32)
    line = jnp.zeros((1, LANES), F32)
    for i in range(pieces):
        tile = arrived_ref[i, rows:].astype(F32)
        recip_ref[i, 0] = 1.0 / (tile[0:1] + tile[1:2] + tile[2:3])
        recip_ref[i, 1] = 1.0 / (tile[3:4] + tile[4:5] + tile[5:6])
        line += tile[6:7] + tile[7:8]
    shift = lax.rem(lax.div(place_ref[0], 2), LANES // share) * share
    inv = lax.rsqrt(as_column(line, share, shift) * (1.0 / D) + EPSILON)
    parts = [total[i * share : (i + 1) * share] for i in range(2 * half // LANES)]
    gate_pre = jnp.concatenate(parts[: half // LANES], axis=1) * inv
    up_pre = jnp.concatenate(parts[half // LANES :], axis=1) * inv
    sigmoid_gate = jax.nn.sigmoid(gate_pre)
    activated = gate_pre * sigmoid_gate
    hidden_act = (activated * up_pre).astype(BF)
    gate_factor = up_pre * sigmoid_gate * (1.0 + gate_pre * (1.0 - sigmoid_gate))
    gate_f_ref[...] = gate_factor * inv
    up_f_ref[...] = activated * inv
    inner_f_ref[...] = (gate_factor * gate_pre + activated * up_pre) * (inv * inv * (1.0 / D))
    for i in range(pieces):
        copies_ref[i] = hidden_act


def down_half(got_ref, feats, half):
    quarter = half // 4
    rows = got_ref[feats : feats + quarter, :]
    return jnp.concatenate([rows[:, i * LANES : (i + 1) * LANES] for i in range(4)], axis=0)


def both_downs(core, down_ref, got_ref):
    feats = down_ref.shape[1]
    half = down_ref.shape[0] // 2
    here = down_ref[half_of(core, half), :]
    return jnp.concatenate([here, down_half(got_ref, feats, half)], axis=1)


def mix(place_ref, act_ref, down_ref, got_ref, pieces_ref):
    core = lax.rem(place_ref[0], 2)
    pieces, share, half = act_ref.shape
    feats = down_ref.shape[1]
    act = act_ref[...].reshape(pieces * share, half)
    shape = pieces_ref.shape[1:]
    mixed = dot(act, both_downs(core, down_ref, got_ref)).astype(BF)
    pieces_ref[core] = mixed[:, :feats].reshape(shape)
    pieces_ref[1 - core] = mixed[:, feats:].reshape(shape)


def finish_outer(arrived_ref, x_ref, final_ref, copies_ref):
    total = x_ref[...].astype(F32)
    for i in range(arrived_ref.shape[0]):
        total += arrived_ref[i].astype(F32)
    scaled = (total * final_ref[...]).astype(BF)
    for i in range(copies_ref.shape[0]):
        copies_ref[i] = scaled


def two_blocks(ref, z, side):
    return jnp.concatenate([ref[z, side], ref[z + 1, side]], axis=0)


def add_features(block_ref, side, wk_ref, wv_ref, recip_ref, keys, values, square):
    for z in range(0, block_ref.shape[0], 2):
        block = jnp.concatenate([block_ref[z], block_ref[z + 1]], axis=1)
        keys += dot(block, two_blocks(wk_ref, z, side))
        values += dot(block, two_blocks(wv_ref, z, side))
        for i in range(2):
            wide = block_ref[z + i].astype(F32) * recip_ref[z + i, side]
            square += wide * wide
    return keys, values, square


def project(place_ref, mine_ref, wk_ref, wv_ref, recip_ref, keys_ref, values_ref, square_ref):
    core = lax.rem(place_ref[0], 2)
    keys_ref[...], values_ref[...], square_ref[...] = add_features(
        mine_ref,
        core,
        wk_ref,
        wv_ref,
        recip_ref,
        jnp.zeros(keys_ref.shape, F32),
        jnp.zeros(values_ref.shape, F32),
        jnp.zeros(square_ref.shape, F32),
    )


def back_to_features(block_ref, side, wk_ref, wv_ref, recip_ref, grads, scales, out_ref):
    key_grad, value_grad = grads
    inv_out, along = scales
    for z in range(0, block_ref.shape[0], 2):
        total = dot(key_grad, two_blocks(wk_ref, z, side), COLS)
        total += dot(value_grad, two_blocks(wv_ref, z, side), COLS)
        for i in range(2):
            recip = recip_ref[z + i, side]
            term = block_ref[z + i].astype(F32) * (recip * recip) * along
            part = total[:, i * LANES : (i + 1) * LANES] * inv_out - term
            out_ref[z + i] = part.astype(out_ref.dtype)


def attend(place_ref, other_ref, wk_ref, wv_ref, recip_ref, keys_ref, values_ref, square_ref, q_ref, g_ref, *outs):
    qg_ref, send_ref, grads_ref, scales_ref, held_ref, sems = outs
    core = lax.rem(place_ref[0], 2)
    rows = other_ref.shape[1]
    scale = HEAD ** (-0.5)
    keys_raw, values_raw, square = add_features(
        other_ref,
        1 - core,
        wk_ref,
        wv_ref,
        recip_ref,
        keys_ref[...],
        values_ref[...],
        square_ref[...],
    )
    inv_out = lax.rsqrt(jnp.sum(square, axis=1, keepdims=True) / D + EPSILON)
    keys = (keys_raw * inv_out).astype(BF)
    values = (values_raw * inv_out).astype(BF)
    scaled_keys = (keys.astype(F32) * scale).astype(BF)
    scaled_values = (values.astype(F32) * scale).astype(BF)
    key_grad = jnp.zeros((rows, HEAD), F32)
    value_grad = jnp.zeros((rows, HEAD), F32)
    step = 256
    leaving = []
    for at in range(0, q_ref.shape[0], step):
        query = q_ref[at : at + step, :]
        grad = g_ref[at : at + step, :]
        scores = dot(scaled_keys, query, COLS)
        raised = jnp.exp(scores - jnp.max(scores, axis=0, keepdims=True))
        probs = raised * (1.0 / jnp.sum(raised, axis=0, keepdims=True))
        probs_bf = probs.astype(BF)
        dprob = dot(scaled_values, grad, COLS)
        delta = jnp.sum(probs_bf.astype(F32) * dprob, axis=0, keepdims=True)
        dscore = (probs * (dprob - delta)).astype(BF)
        part = pl.ds(at, step)
        held_ref[part, :] = dot(dscore, keys, ROWS).astype(BF)
        leaving.append(
            pltpu.make_async_copy(held_ref.at[part, :], qg_ref.at[part, :], sems.at[at // step])
        )
        leaving[-1].start()
        key_grad += dot(dscore, query)
        value_grad += dot(probs_bf, grad)
    key_grad = key_grad.astype(BF)
    value_grad = value_grad.astype(BF)
    inner = jnp.sum(
        key_grad.astype(F32) * keys_raw + value_grad.astype(F32) * values_raw, axis=1, keepdims=True
    )
    along = inv_out * inv_out * inv_out * inner * (1.0 / D)
    grads_ref[0] = key_grad
    grads_ref[1] = value_grad
    scales_ref[0] = jnp.broadcast_to(inv_out, (rows, LANES))
    scales_ref[1] = jnp.broadcast_to(along, (rows, LANES))
    grads = (key_grad, value_grad)
    scales = (inv_out, along)
    back_to_features(other_ref, 1 - core, wk_ref, wv_ref, recip_ref, grads, scales, send_ref)
    for copy in leaving:
        copy.wait()


def keep_own(place_ref, mine_ref, wk_ref, wv_ref, recip_ref, grads_ref, scales_ref, keep_ref):
    core = lax.rem(place_ref[0], 2)
    grads = (grads_ref[0], grads_ref[1])
    scales = (scales_ref[0], scales_ref[1])
    back_to_features(mine_ref, core, wk_ref, wv_ref, recip_ref, grads, scales, keep_ref)


def outer_gradient(arrived_ref, final_ref, grad_ref, copies_ref):
    totals = [arrived_ref[i].astype(F32) for i in range(8)]
    for i in range(8, arrived_ref.shape[0]):
        totals[i % 8] += arrived_ref[i].astype(F32)
    total = sum(totals[1:], totals[0]) * final_ref[...]
    grad_ref[...] = total
    rounded = total.astype(BF)
    for i in range(copies_ref.shape[0]):
        copies_ref[i] = rounded


def through_down(place_ref, outer_ref, down_ref, got_ref, pieces_ref):
    core = lax.rem(place_ref[0], 2)
    outer = jnp.concatenate([outer_ref[core], outer_ref[1 - core]], axis=1)
    part = dot(outer, both_downs(core, down_ref, got_ref), COLS)
    pieces_ref[...] = part.astype(BF).reshape(pieces_ref.shape)


def gate_up_gradient(arrived_ref, gate_f_ref, up_f_ref, inner_f_ref, copies_ref):
    half = gate_f_ref.shape[1]
    total = arrived_ref[0].astype(F32)
    for i in range(1, arrived_ref.shape[0]):
        total += arrived_ref[i].astype(F32)
    gate = in_blocks((total * gate_f_ref[...]).astype(BF))
    up = in_blocks((total * up_f_ref[...]).astype(BF))
    inner = jnp.sum(total * inner_f_ref[...], axis=1, keepdims=True)
    line = jnp.sum(jnp.where(diagonal(inner.shape[0], 0), inner, 0.0), axis=0, keepdims=True)
    high = line.astype(BF).astype(F32)
    tile = by_row((high, line - high), 16).astype(BF)
    rows = gate.shape[0]
    for i in range(copies_ref.shape[0]):
        copies_ref[i, :rows] = gate
        copies_ref[i, rows : 2 * rows] = up
        copies_ref[i, 2 * rows :] = tile


def columns_of(grads_ref, at, width, whole):
    share = (grads_ref.shape[1] - 16) * LANES // whole
    blocks = range(at // LANES, (at + width) // LANES)
    tokens = grads_ref.shape[0] * share
    parts = [grads_ref[:, i * share : (i + 1) * share].reshape(tokens, LANES) for i in blocks]
    return jnp.concatenate(parts, axis=1)


def through_gate_up(place_ref, grads_ref, x_ref, mlp_ref, gate_ref, up_ref, got_ref, pieces_ref):
    core = lax.rem(place_ref[0], 2)
    half = gate_ref.shape[1] // 2
    feats = gate_ref.shape[0]
    here = half_of(core, half)
    tokens = x_ref.shape[1]
    shape = pieces_ref.shape[1:]
    weights = jnp.concatenate([gate_ref[:, here], up_ref[:, here]], axis=1)
    weights = jnp.concatenate([weights, got_ref[:feats, :]], axis=0)
    total = dot(columns_of(grads_ref, 0, 2 * half, 2 * half), weights, COLS)
    share = tokens // grads_ref.shape[0]
    lines = [grads_ref[i, grads_ref.shape[1] - 16 :].astype(F32) for i in range(grads_ref.shape[0])]
    inner = jnp.concatenate([as_column(v[0:1] + v[1:2], share) for v in lines], axis=0)
    part = total[:, :feats] * mlp_ref[...] - x_ref[core].astype(F32) * inner
    pieces_ref[core] = part.astype(BF).reshape(shape)
    mlp_there, _ = got_gains(got_ref, feats + half // 4)
    part = total[:, feats:] * mlp_there - x_ref[1 - core].astype(F32) * inner
    pieces_ref[1 - core] = part.astype(BF).reshape(shape)


def finish(place_ref, scaled_ref, here_ref, there_ref, normed_ref, outer_ref, gate_ref, up_ref, grad_ref):
    core = lax.rem(place_ref[0], 2)
    half = gate_ref.shape[1] // 2
    scaled = scaled_ref[...]
    columns = [columns_of(ref, 0, 2 * half, 2 * half) for ref in (here_ref, there_ref)]
    both = dot(scaled, jnp.concatenate(columns, axis=1), ROWS).astype(BF)
    for i, place in enumerate((core, 1 - core)):
        at = half_of(place, half)
        gate_ref[:, at] = both[:, 2 * i * half : (2 * i + 1) * half]
        up_ref[:, at] = both[:, (2 * i + 1) * half : (2 * i + 2) * half]
    grad_ref[...] = outer_ref[...] + normed_ref[...]


def down_weights(place_ref, outer_ref, here_ref, there_ref, down_ref):
    core = lax.rem(place_ref[0], 2)
    half = down_ref.shape[0] // 2
    tokens = outer_ref.shape[1]
    outer = outer_ref[core]
    for act_ref, place in ((here_ref, core), (there_ref, 1 - core)):
        act = act_ref[...].reshape(tokens, half)
        down_ref[half_of(place, half), :] = dot(act, outer, ROWS).astype(BF)


def call(body, outs, *args, flops=0, first_out=None, scratch=()):
    vmem = pl.BlockSpec(memory_space=pltpu.VMEM)
    in_specs = [vmem] * len(args)
    if args[0].dtype == jnp.int32:
        in_specs[0] = pl.BlockSpec(memory_space=pltpu.SMEM)
    shapes = tuple(jax.ShapeDtypeStruct(shape, dtype) for shape, dtype in outs)
    moved = sum(a.size * a.dtype.itemsize for a in (*args, *shapes))
    results = pl.pallas_call(
        body,
        out_shape=shapes,
        in_specs=in_specs,
        out_specs=(first_out or vmem,) + (vmem,) * (len(shapes) - 1),
        scratch_shapes=scratch,
        compiler_params=pltpu.CompilerParams(vmem_limit_bytes=40 * 1024 * 1024),
        cost_estimate=pl.CostEstimate(flops=flops, bytes_accessed=moved, transcendentals=0),
    )(*args)
    return results


def on_device(
    enc_hidden,
    mlp_gain,
    final_gain,
    w_gate,
    w_up,
    w_down,
    key_weight,
    value_weight,
    queries,
    context_grad,
):
    block, feats = enc_hidden.shape
    half = w_gate.shape[1] // 2
    place = (2 * lax.axis_index("z") + lax.axis_index("core")).astype(jnp.int32).reshape(1)
    chips = lax.axis_size("z")
    blocks = lax.axis_size("tensor")
    tokens = block * blocks
    share = tokens // chips
    mlp_gain = mlp_gain.reshape(1, feats)
    final_gain = final_gain.reshape(1, feats)

    piece = share * 2 * half // LANES + 16

    (copies,) = call(spread, [((2 * blocks, block, feats), BF)], enc_hidden)
    hidden = exchange(copies, WIDE).reshape(2, tokens, feats)
    (sent,) = call(
        start,
        [((feats + half // 4 + 16, 2 * half), BF)],
        place, mlp_gain, final_gain, w_gate, w_up, w_down,
    )
    got = other_core(sent)
    pieces, scaled = call(
        gate_up,
        [((chips, piece, LANES), BF), ((tokens, feats), BF)],
        place, hidden, mlp_gain, final_gain, w_gate, w_up, got,
    )
    arrived = exchange(pieces, "z")
    copies, gate_f, up_f, inner_f, recip = call(
        activate,
        [((chips, share, half), BF)]
        + [((share, half), F32)] * 3
        + [((chips, 2, 1, LANES), F32)],
        place, arrived,
    )
    act = exchange(copies, "z")
    act_there = other_core(act)
    (pieces,) = call(
        mix, [((2, blocks, block, feats), BF)], place, act, w_down, got
    )
    arrived = exchange(pieces.reshape(-1, block, feats), WIDE)
    (copies,) = call(
        finish_outer, [((chips * blocks, block, feats), BF)], arrived, enc_hidden, final_gain
    )
    mine = exchange(copies, ("z", "tensor")).reshape(chips, tokens, feats)
    other = other_core(mine)
    by_block = (chips, 2, LANES, HEAD)
    weights = (key_weight.reshape(by_block), value_weight.reshape(by_block), recip)
    projected = call(
        project,
        [((tokens, HEAD), F32)] * 2 + [((tokens, LANES), F32)],
        place, mine, *weights,
        flops=270_000_000,
    )
    query_grad, send, layer_grads, scales = call(
        attend,
        [
            (queries.shape[1:], BF),
            (mine.shape, BF),
            ((2, tokens, HEAD), BF),
            ((2, tokens, LANES), F32),
        ],
        place, other, *weights, *projected, queries[0], context_grad[0],
        flops=1_200_000_000,
        first_out=pl.BlockSpec(memory_space=pl.ANY),
        scratch=[pltpu.VMEM(queries.shape[1:], BF), pltpu.SemaphoreType.DMA((4,))],
    )
    (keep,) = call(
        keep_own, [(mine.shape, F32)], place, mine, *weights, layer_grads, scales, flops=270_000_000
    )
    both = (keep + other_core(send).astype(F32)).astype(BF)
    arrived = exchange(both.reshape(-1, block, feats), ("z", "tensor"))
    outer_grad, copies = call(
        outer_gradient,
        [((block, feats), F32), ((2 * blocks, block, feats), BF)],
        arrived, final_gain,
    )
    outer = exchange(copies, WIDE).reshape(2, tokens, feats)
    (pieces,) = call(through_down, [((chips, share, half), BF)], place, outer, w_down, got)
    arrived = exchange(pieces, "z")
    (down_weight_grad,) = call(down_weights, [(w_down.shape, BF)], place, outer, act, act_there)
    (copies,) = call(
        gate_up_gradient, [((chips, piece, LANES), BF)], arrived, gate_f, up_f, inner_f
    )
    grads = exchange(copies, "z")
    grads_there = other_core(grads)
    (pieces,) = call(
        through_gate_up,
        [((2, blocks, block, feats), BF)],
        place, grads, hidden, mlp_gain, w_gate, w_up, got,
    )
    arrived = exchange(pieces.reshape(-1, block, feats), WIDE)
    gate_weight_grad, up_weight_grad, hidden_grad = call(
        finish,
        [(w_gate.shape, BF), (w_up.shape, BF), ((block, feats), F32)],
        place, scaled, grads, grads_there, arrived.astype(F32).sum(axis=0), outer_grad,
    )
    return (query_grad[None], hidden_grad, gate_weight_grad, up_weight_grad, down_weight_grad)


def solution(mesh):
    names = list(mesh.axis_names)
    at = names.index("section")
    shape = list(mesh.devices.shape)
    names[at : at + 1] = SECTION
    shape[at : at + 1] = [shape[at] // 2, 2]
    fine = Mesh(mesh.devices.reshape(shape), tuple(names))
    in_specs = (
        P(("dp", "tensor"), SECTION),
        P(SECTION),
        P(SECTION),
        P(SECTION, "tensor"),
        P(SECTION, "tensor"),
        P("tensor", SECTION),
        P(SECTION, None, "tensor"),
        P(SECTION, None, "tensor"),
        P(SECTION, "dp", "tensor"),
        P(SECTION, "dp", "tensor"),
    )
    out_specs = (
        P(SECTION, "dp", "tensor"),
        P(("dp", "tensor"), SECTION),
        P(("dp", *SECTION), "tensor"),
        P(("dp", *SECTION), "tensor"),
        P(("dp", "tensor"), SECTION),
    )
    return jax.shard_map(
        on_device, mesh=fine, in_specs=in_specs, out_specs=out_specs, check_vma=False
    )
```
